32 devices in a mesh: dp: 8 (over z, x), seq: 4 (over y, core).
Axes of the slice: x: 2, y: 2, z: 4, core: 2. Of those that a mesh axis runs over, the one named last changes fastest.
Arguments:
- tokens: bfloat16 [8, 2048, 1024], P('dp', 'seq'), may hold values from -6 to 6
- cotangent: bfloat16 [8, 2048, 1024], P('dp', 'seq'), may hold values from -6 to 6
- w_qkv: bfloat16 [1024, 3072], P('dp'), may hold values from -0.1875 to 0.1875
- w_attn: bfloat16 [1024, 1024], P('dp'), may hold values from -1.5 to 1.5
- w_fc: bfloat16 [1024, 4096], P('dp'), may hold values from -0.1875 to 0.1875
- w_proj: bfloat16 [4096, 1024], P('dp'), may hold values from -0.09375 to 0.09375
- bias_query: bfloat16 [1024], P('dp'), may hold values from -3 to 3
- bias_value: bfloat16 [1024], P('dp'), may hold values from -3 to 3
- bias_attn: bfloat16 [1024], P('dp'), may hold values from -3 to 3
- gain_one: bfloat16 [1024], P('dp'), may hold values from 0.5 to 1.5
- shift_one: bfloat16 [1024], P('dp'), may hold values from -3 to 3
- gain_two: bfloat16 [1024], P('dp'), may hold values from 0.5 to 1.5
- shift_two: bfloat16 [1024], P('dp'), may hold values from -3 to 3
- bias_fc: bfloat16 [4096], P('dp'), may hold values from -3 to 3
- bias_proj: bfloat16 [1024], P('dp'), may hold values from -3 to 3
Outputs:
- output: bfloat16 [8, 2048, 1024], P('dp', 'seq')
- grad_tokens: float32 [8, 2048, 1024], P('dp', 'seq')
- grad_w_qkv: float32 [1024, 3072], P('dp')
- grad_w_attn: float32 [1024, 1024], P('dp')
- grad_w_fc: float32 [1024, 4096], P('dp')
- grad_w_proj: float32 [4096, 1024], P('dp')
- grad_bias_query: float32 [1024], P('dp')
- grad_bias_value: float32 [1024], P('dp')
- grad_bias_attn: float32 [1024], P('dp')
- grad_gain_one: float32 [1024], P('dp')
- grad_shift_one: float32 [1024], P('dp')
- grad_gain_two: float32 [1024], P('dp')
- grad_shift_two: float32 [1024], P('dp')
- grad_bias_fc: float32 [4096], P('dp')
- grad_bias_proj: float32 [1024], P('dp')
The draws below stay inside these ranges and needn't reach their ends.
All inputs are finite; a program needn't handle non-finite values.
Results may differ from the reference program's by a relative error of at most 0.018.
Values may be sent and summed in bfloat16 or wider, within the bound.
No kernel may reach another device: no remote copies, remote signals or barrier semaphores. Data moves between devices by JAX's collectives and lax.ppermute only.
A program may use at most 256 MiB of HBM per device.

```python
import math
import jax
import jax.numpy as jnp
from jax import lax

D = 1024
FF = 4096
HEADS = 16
HEAD_DIM = 64
ROW_BLOCK = 512
LENGTH = 2048
BATCH = 8


def levels(own_key, extent, shards, smallest, top_value):
    level = 1.0
    for position, blocks in shards:
        steps = jax.random.uniform(jax.random.fold_in(jax.random.fold_in(own_key, 6), position), (blocks,), jnp.float32, smallest / len(shards), top_value / len(shards))
        level = level * jnp.repeat(jnp.exp(steps), extent[position] // blocks).reshape((-1,) + (1,) * (len(extent) - 1 - position))
    return level


def gaussian(key, extent, deviation, reach, pieces=(), kind=jnp.bfloat16):
    gain = levels(key, extent, pieces, -0.22, 0.18) if pieces else 1.0
    drawn = jax.random.normal(key, extent, jnp.float32) * deviation * gain
    return jnp.minimum(jnp.maximum(drawn, -reach), reach).astype(kind)


def setup_inputs(seed: int = 0) -> dict:
    seeds = jax.random.split(jax.random.key(seed), 16)
    tokens = gaussian(seeds[0], (BATCH, LENGTH, D), 1.0, 6.0, ((0, 8), (1, 4)))
    cotangent = gaussian(seeds[1], (BATCH, LENGTH, D), 1.0, 6.0, ((0, 8), (1, 4)))
    w_qkv = gaussian(seeds[2], (D, 3 * D), D ** -0.5, 0.1875, ((0, 8),))
    w_attn = gaussian(seeds[3], (D, D), (D // 64) ** -0.5, 1.5, ((0, 8),))
    w_fc = gaussian(seeds[4], (D, FF), D ** -0.5, 0.1875, ((0, 8),))
    w_proj = gaussian(seeds[5], (FF, D), FF ** -0.5, 0.09375, ((0, 8),))
    bias_query = gaussian(seeds[6], (D,), 0.3, 3.0, ((0, 8),))
    bias_value = gaussian(seeds[7], (D,), 0.3, 3.0, ((0, 8),))
    bias_attn = gaussian(seeds[8], (D,), 0.3, 3.0, ((0, 8),))
    gain_one = jnp.clip(1.0 + 0.1 * jax.random.normal(seeds[9], (D,), jnp.float32), 0.5, 1.5).astype(jnp.bfloat16)
    shift_one = gaussian(seeds[10], (D,), 0.3, 3.0, ((0, 8),))
    gain_two = jnp.clip(1.0 + 0.1 * jax.random.normal(seeds[11], (D,), jnp.float32), 0.5, 1.5).astype(jnp.bfloat16)
    shift_two = gaussian(seeds[12], (D,), 0.3, 3.0, ((0, 8),))
    bias_fc = gaussian(seeds[13], (FF,), 0.3, 3.0, ((0, 8),))
    bias_proj = gaussian(seeds[14], (D,), 0.3, 3.0, ((0, 8),))
    return {"tokens": tokens, "cotangent": cotangent, "w_qkv": w_qkv, "w_attn": w_attn, "w_fc": w_fc, "w_proj": w_proj, "bias_query": bias_query, "bias_value": bias_value, "bias_attn": bias_attn, "gain_one": gain_one, "shift_one": shift_one, "gain_two": gain_two, "shift_two": shift_two, "bias_fc": bias_fc, "bias_proj": bias_proj}


EPSILON = 1e-05
ROOT_COEF = 0.7978845608028654
HIGHEST = lax.Precision.HIGHEST

@jax.custom_vjp
def low(v):
    return lax.optimization_barrier(v.astype(jnp.bfloat16)).astype(jnp.float32)

@jax.custom_vjp
def low_back(v):
    return v

def low_keep(v):
    return (low(v), None)

def low_pass(kept, grad):
    return (grad,)

def back_keep(v):
    return (v, None)

def back_low(kept, grad):
    return (low(grad),)
low.defvjp(low_keep, low_pass)
low_back.defvjp(back_keep, back_low)

def layer_norm(values, gain_vec, shift_vec):
    average = lax.optimization_barrier(jnp.mean(values, axis=-1, keepdims=True))
    centered = values - average
    variance = lax.optimization_barrier(jnp.mean(centered * centered, axis=-1, keepdims=True))
    return centered * lax.rsqrt(variance + EPSILON) * gain_vec + shift_vec

def gelu_tanh(values):
    return 0.5 * values * (1.0 + jnp.tanh(ROOT_COEF * (values + 0.044715 * values * values * values)))

def product(left_side, right_side):
    return jnp.dot(left_side, right_side, precision=HIGHEST, preferred_element_type=jnp.float32)

def both_ways(values):
    return low(low_back(values))

def attend_block(query_block, key_rows, value_rows, start):
    scores = jnp.einsum('gqhd,gkhd->ghqk', query_block, key_rows, precision=HIGHEST) * HEAD_DIM ** (-0.5)
    scores = low_back(scores)
    row_pos = start + jnp.arange(ROW_BLOCK, dtype=jnp.int32)
    col_pos = jnp.arange(LENGTH, dtype=jnp.int32)
    allowed = row_pos[:, None] >= col_pos[None, :]
    scores = jnp.where(allowed, scores, -1e+30)
    probability = low(jax.nn.softmax(scores, axis=-1))
    return jnp.einsum('ghqk,gkhd->gqhd', probability, value_rows, precision=HIGHEST)

def attend(query_rows, key_rows, value_rows):
    block_count = LENGTH // ROW_BLOCK
    groups = query_rows.shape[0]
    blocks = query_rows.reshape(groups, block_count, ROW_BLOCK, HEADS, HEAD_DIM).transpose(1, 0, 2, 3, 4)
    starts = jnp.arange(block_count, dtype=jnp.int32) * ROW_BLOCK

    def one_block(block_pair):
        return attend_block(block_pair[0], key_rows, value_rows, block_pair[1])
    results = lax.map(jax.checkpoint(one_block), (blocks, starts))
    return results.transpose(1, 0, 2, 3, 4).reshape(groups, LENGTH, D)

def forward(inputs, w_qkv, w_attn, w_fc, w_proj, bias_query, bias_value, bias_attn, gain_one, shift_one, gain_two, shift_two, bias_fc, bias_proj):
    groups = inputs.shape[0]
    normed = low(layer_norm(inputs, gain_one, shift_one))
    mixed_rows = product(normed, w_qkv)
    query_rows = both_ways(mixed_rows[..., :D] + bias_query)
    key_rows = both_ways(mixed_rows[..., D:2 * D])
    value_rows = both_ways(mixed_rows[..., 2 * D:] + bias_value)
    head_shape = (groups, LENGTH, HEADS, HEAD_DIM)
    attended = both_ways(attend(query_rows.reshape(head_shape), key_rows.reshape(head_shape), value_rows.reshape(head_shape)))
    branch = low_back(product(attended, w_attn) + bias_attn)
    middle = inputs + branch
    normed_two = low(layer_norm(middle, gain_two, shift_two))
    hidden = low_back(product(normed_two, w_fc) + bias_fc)
    active = low(gelu_tanh(hidden))
    return middle + product(active, w_proj) + bias_proj

def reference(tokens, cotangent, w_qkv, w_attn, w_fc, w_proj, bias_query, bias_value, bias_attn, gain_one, shift_one, gain_two, shift_two, bias_fc, bias_proj):
    params = tuple((item.astype(jnp.float32) for item in (w_qkv, w_attn, w_fc, w_proj, bias_query, bias_value, bias_attn, gain_one, shift_one, gain_two, shift_two, bias_fc, bias_proj)))
    pack = math.gcd(BATCH, max(1, 4096 // LENGTH))
    group_tokens = tokens.astype(jnp.float32).reshape(BATCH // pack, pack, LENGTH, D)
    group_cotangent = cotangent.astype(jnp.float32).reshape(BATCH // pack, pack, LENGTH, D)

    def scan_step(totals_carry, group_pair):
        result, pullback = jax.vjp(forward, group_pair[0], *params)
        gradients = pullback(group_pair[1])
        totals_carry = tuple((acc + grad for acc, grad in zip(totals_carry, gradients[1:])))
        return (totals_carry, (result.astype(jnp.bfloat16), gradients[0]))
    initial = tuple((jnp.zeros_like(item) for item in params))
    totals_carry, (outputs, grad_inputs) = lax.scan(scan_step, initial, (group_tokens, group_cotangent))
    output = outputs.reshape(BATCH, LENGTH, D)
    grad_tokens = grad_inputs.reshape(BATCH, LENGTH, D)
    grad_w_qkv, grad_w_attn, grad_w_fc, grad_w_proj, grad_bias_query, grad_bias_value, grad_bias_attn, grad_gain_one, grad_shift_one, grad_gain_two, grad_shift_two, grad_bias_fc, grad_bias_proj = totals_carry
    return (output, grad_tokens, grad_w_qkv, grad_w_attn, grad_w_fc, grad_w_proj, grad_bias_query, grad_bias_value, grad_bias_attn, grad_gain_one, grad_shift_one, grad_gain_two, grad_shift_two, grad_bias_fc, grad_bias_proj)
```

```python
import functools

import jax
import jax.numpy as jnp
from jax import lax
from jax.experimental import pallas as pl
from jax.experimental.pallas import tpu as pltpu
from jax.sharding import PartitionSpec as P

HEAD_DIM = 64
EPSILON = 1e-05
ROOT_COEF = 0.7978845608028654
SCALE = HEAD_DIM ** (-0.5)
BF16 = jnp.bfloat16
F32 = jnp.float32
LOG_ROWS = 8
VMEM_BYTES = 56 * 1024 * 1024


def gelu_tanh(values):
    return (
        0.5 * values * (1.0 + jnp.tanh(ROOT_COEF * (values + 0.044715 * values * values * values)))
    )


def dot_nn(left_side, right_side):
    return lax.dot_general(
        left_side, right_side, (((1,), (0,)), ((), ())), preferred_element_type=F32
    )


def dot_nt(left_side, right_side):
    return lax.dot_general(
        left_side, right_side, (((1,), (1,)), ((), ())), preferred_element_type=F32
    )


def dot_tn(left_side, right_side):
    return lax.dot_general(
        left_side, right_side, (((0,), (0,)), ((), ())), preferred_element_type=F32
    )


def head_lanes(array, head):
    lanes = lax.broadcasted_iota(jnp.int32, array.shape, 1)
    owner = lax.shift_right_logical(lanes, 6)
    return jnp.where(owner == head, array.astype(F32), 0.0)


def attend_kernel(mixed_ref, out_ref, log_ref, *, block, width):
    length = mixed_ref.shape[1]
    heads = width // HEAD_DIM
    step = 2 if heads % 2 == 0 else 1
    for index in range(length // block):
        first, stop = index * block, (index + 1) * block
        query = mixed_ref[0, first:stop, 0:width]
        row_pos = lax.broadcasted_iota(jnp.int32, (block, block), 0)
        col_pos = lax.broadcasted_iota(jnp.int32, (block, block), 1)
        allowed = row_pos >= col_pos
        log_lanes = lax.broadcasted_iota(jnp.int32, (block, 128), 1)

        def one_head(head, carry):
            total, logs = carry
            masked = (head_lanes(query, head) * SCALE).astype(BF16)
            diagonal = dot_nt(masked, mixed_ref[0, first:stop, width : 2 * width])
            diagonal = jnp.where(allowed, diagonal, -1e30)
            largest = jnp.max(diagonal, axis=1, keepdims=True)
            if first:
                scores = dot_nt(masked, mixed_ref[0, 0:first, width : 2 * width])
                largest = jnp.maximum(largest, jnp.max(scores, axis=1, keepdims=True))
            weights = jnp.exp(diagonal - largest)
            row_total = jnp.sum(weights, axis=1, keepdims=True)
            mixed = dot_nn(
                weights.astype(BF16), mixed_ref[0, first:stop, 2 * width : 3 * width]
            )
            if first:
                weights = jnp.exp(scores - largest)
                row_total = row_total + jnp.sum(weights, axis=1, keepdims=True)
                mixed = mixed + dot_nn(
                    weights.astype(BF16), mixed_ref[0, 0:first, 2 * width : 3 * width]
                )
            total = total + head_lanes(mixed * (1.0 / row_total), head)
            logs = jnp.where(log_lanes == head, largest + jnp.log(row_total), logs)
            return (total, logs)

        def some_heads(group, carry):
            for inner in range(step):
                carry = one_head(group * step + inner, carry)
            return carry

        total, logs = lax.fori_loop(
            0,
            heads // step,
            some_heads,
            (jnp.zeros((block, width), F32), jnp.zeros((block, 128), F32)),
        )
        out_ref[0, first:stop, :] = total.astype(BF16)
        log_ref[0, :, first:stop] = jnp.transpose(logs)[0:LOG_ROWS]


def attend(mixed, width):
    seqs, length, _ = mixed.shape
    block = min(256, length)
    return pl.pallas_call(
        functools.partial(attend_kernel, block=block, width=width),
        grid=(seqs,),
        in_specs=[pl.BlockSpec((1, length, 3 * width), lambda s: (s, 0, 0))],
        out_specs=[
            pl.BlockSpec((1, length, width), lambda s: (s, 0, 0)),
            pl.BlockSpec((1, LOG_ROWS, length), lambda s: (s, 0, 0)),
        ],
        out_shape=[
            jax.ShapeDtypeStruct((seqs, length, width), BF16),
            jax.ShapeDtypeStruct((seqs, LOG_ROWS, length), F32),
        ],
        compiler_params=pltpu.CompilerParams(vmem_limit_bytes=VMEM_BYTES),
        cost_estimate=pl.CostEstimate(
            flops=4 * seqs * length * length * width,
            bytes_accessed=8 * seqs * length * width,
            transcendentals=seqs * length * length * width // HEAD_DIM // 2,
        ),
    )(mixed)


def attend_back_kernel(
    mixed_ref,
    out_ref,
    grad_ref,
    log_ref,
    result_ref,
    query_heads,
    key_heads,
    grad_heads,
    grad_query,
    grad_key,
    grad_value,
    inner_rows,
    *,
    block,
    width,
):
    length = mixed_ref.shape[1]
    heads = width // HEAD_DIM
    blocks = length // block
    owner = lax.shift_right_logical(lax.broadcasted_iota(jnp.int32, (LOG_ROWS, width), 1), 6)
    picks = (owner == lax.broadcasted_iota(jnp.int32, (LOG_ROWS, width), 0)).astype(F32)

    def prepare(index, carry):
        rows = pl.ds(pl.multiple_of(index * block, block), block)
        query = mixed_ref[0, rows, 0:width]
        key = mixed_ref[0, rows, width : 2 * width]
        grad = grad_ref[0, rows, :]
        for head in range(heads):
            query_heads[head, rows, :] = (head_lanes(query, head) * SCALE).astype(BF16)
            key_heads[head, rows, :] = head_lanes(key, head).astype(BF16)
            grad_heads[head, rows, :] = head_lanes(grad, head).astype(BF16)
        product = grad.astype(F32) * out_ref[0, rows, :].astype(F32)
        inner_rows[:, rows] = lax.dot_general(
            picks,
            product,
            (((1,), (1,)), ((), ())),
            precision=lax.Precision.HIGHEST,
            preferred_element_type=F32,
        )
        zeros = jnp.zeros((block, width), F32)
        grad_query[rows, :] = zeros
        grad_key[rows, :] = zeros
        grad_value[rows, :] = zeros
        return carry

    lax.fori_loop(0, blocks, prepare, 0)

    def tile(row_block, col_block, on_diagonal):
        rows = pl.ds(pl.multiple_of(row_block * block, block), block)
        cols = pl.ds(pl.multiple_of(col_block * block, block), block)
        key = mixed_ref[0, cols, width : 2 * width]
        value = mixed_ref[0, cols, 2 * width : 3 * width]
        add_query = add_key = add_value = None
        for head in range(heads):
            query = query_heads[head, rows, :]
            grad = grad_heads[head, rows, :]
            probs = jnp.exp(dot_nt(key, query) - log_ref[0, head : head + 1, rows])
            if on_diagonal:
                key_pos = lax.broadcasted_iota(jnp.int32, (block, block), 0)
                row_pos = lax.broadcasted_iota(jnp.int32, (block, block), 1)
                probs = jnp.where(row_pos >= key_pos, probs, 0.0)
            grad_probs = dot_nt(value, grad)
            grad_scores = (probs * (grad_probs - inner_rows[head : head + 1, rows])).astype(BF16)
            one_value = dot_nn(probs.astype(BF16), grad)
            one_key = dot_nn(grad_scores, query)
            one_query = dot_tn(grad_scores, key_heads[head, cols, :])
            add_value = one_value if head == 0 else add_value + one_value
            add_key = one_key if head == 0 else add_key + one_key
            add_query = one_query if head == 0 else add_query + one_query
        grad_value[cols, :] += add_value
        grad_key[cols, :] += add_key
        grad_query[rows, :] += add_query

    def row_step(row_block, carry):
        def col_step(col_block, inner_carry):
            tile(row_block, col_block, False)
            return inner_carry

        lax.fori_loop(0, row_block, col_step, 0)
        tile(row_block, row_block, True)
        return carry

    lax.fori_loop(0, blocks, row_step, 0)

    def finish(index, carry):
        rows = pl.ds(pl.multiple_of(index * block, block), block)
        result_ref[0, rows, 0:width] = (grad_query[rows, :] * SCALE).astype(BF16)
        result_ref[0, rows, width : 2 * width] = grad_key[rows, :].astype(BF16)
        result_ref[0, rows, 2 * width : 3 * width] = grad_value[rows, :].astype(BF16)
        return carry

    lax.fori_loop(0, blocks, finish, 0)


def attend_back(mixed, attended, grad_attended, logs, width):
    seqs, length, _ = mixed.shape
    heads = width // HEAD_DIM
    block = min(256, length)
    return pl.pallas_call(
        functools.partial(attend_back_kernel, block=block, width=width),
        grid=(seqs,),
        in_specs=[
            pl.BlockSpec((1, length, 3 * width), lambda s: (s, 0, 0)),
            pl.BlockSpec((1, length, width), lambda s: (s, 0, 0)),
            pl.BlockSpec((1, length, width), lambda s: (s, 0, 0)),
            pl.BlockSpec((1, LOG_ROWS, length), lambda s: (s, 0, 0)),
        ],
        out_specs=pl.BlockSpec((1, length, 3 * width), lambda s: (s, 0, 0)),
        out_shape=jax.ShapeDtypeStruct((seqs, length, 3 * width), BF16),
        scratch_shapes=[
            pltpu.VMEM((heads, length, width), BF16),
            pltpu.VMEM((heads, length, width), BF16),
            pltpu.VMEM((heads, length, width), BF16),
            pltpu.VMEM((length, width), F32),
            pltpu.VMEM((length, width), F32),
            pltpu.VMEM((length, width), F32),
            pltpu.VMEM((LOG_ROWS, length), F32),
        ],
        compiler_params=pltpu.CompilerParams(vmem_limit_bytes=VMEM_BYTES),
        cost_estimate=pl.CostEstimate(
            flops=10 * seqs * length * length * width,
            bytes_accessed=16 * seqs * length * width,
            transcendentals=seqs * length * length * width // HEAD_DIM // 2,
        ),
    )(mixed, attended, grad_attended, logs)


def swap(array, offset):
    ranks = lax.axis_size("seq")
    return lax.ppermute(array, "seq", [(rank, rank ^ offset) for rank in range(ranks)])


def bits_up():
    ranks, bits, bit = (lax.axis_size("seq"), [], 1)
    while bit < ranks:
        bits.append(bit)
        bit *= 2
    return bits


def gather_offsets(array):
    found = {0: array}
    for bit in reversed(bits_up()):
        for offset in sorted(found):
            found[offset | bit] = swap(found[offset], bit)
    return [found[offset] for offset in range(len(found))]


def reduce_offsets(blocks):
    left = dict(enumerate(blocks))
    for bit in bits_up():
        for offset in sorted(left, reverse=True):
            if offset & bit:
                arrived = swap(left.pop(offset).astype(BF16), bit)
                left[offset ^ bit] = left[offset ^ bit].astype(F32) + arrived.astype(F32)
    return left[0]


def in_rank_order(blocks):
    rank = lax.axis_index("seq")
    stacked = jnp.zeros((len(blocks),) + blocks[0].shape, blocks[0].dtype)
    for offset, block in enumerate(blocks):
        stacked = lax.dynamic_update_index_in_dim(stacked, block, rank ^ offset, 0)
    return stacked


def by_offset(array, axis):
    rank = lax.axis_index("seq")
    ranks = array.shape[axis]
    return [
        lax.dynamic_index_in_dim(array, rank ^ offset, axis, keepdims=False)
        for offset in range(ranks)
    ]


def row_stats(values):
    average = jnp.mean(values, axis=-1, keepdims=True)
    centered = values - average
    variance = jnp.mean(centered * centered, axis=-1, keepdims=True)
    inverse = lax.rsqrt(variance + EPSILON)
    return centered * inverse, inverse


def norm_back(incoming, gain, unit, inverse):
    scaled = incoming * gain
    first = jnp.mean(scaled, axis=-1, keepdims=True)
    second = jnp.mean(scaled * unit, axis=-1, keepdims=True)
    return inverse * (scaled - first - unit * second)


def pad_rows(array, multiple):
    rows = array.shape[0]
    return jnp.pad(array, ((0, -rows % multiple), (0, 0)))


def vector_rows(vectors, parts, columns):
    flat = jnp.concatenate([item.reshape(parts, -1) for item in vectors], axis=1)
    size = flat.shape[1]
    rows = -(-size // columns)
    rows = -(-rows // 16) * 16
    flat = jnp.pad(flat, ((0, 0), (0, rows * columns - size)))
    return flat.reshape(parts, rows, columns)


def per_device(
    tokens,
    cotangent,
    w_qkv,
    w_attn,
    w_fc,
    w_proj,
    bias_query,
    bias_value,
    bias_attn,
    gain_one,
    shift_one,
    gain_two,
    shift_two,
    bias_fc,
    bias_proj,
):
    ranks = lax.axis_size("seq")
    shards = lax.axis_size("dp")
    rank = lax.axis_index("seq")
    seqs, rows, model = tokens.shape
    length = rows * ranks
    width = model // ranks
    part = w_qkv.shape[0]
    hidden_part = w_proj.shape[0]
    units = hidden_part // ranks
    hidden_width = w_fc.shape[1] // ranks
    tokens_own = tokens.reshape(seqs * rows, model)
    cot_own = cotangent.reshape(seqs * rows, model)

    qkv_share = lax.dynamic_index_in_dim(
        w_qkv.reshape(part, 3, ranks, width), rank, 2, keepdims=False
    ).reshape(part, 3 * width)
    vectors = (
        bias_query,
        bias_value,
        bias_attn,
        gain_one,
        shift_one,
        gain_two,
        shift_two,
        bias_proj,
        bias_fc,
    )
    packed = jnp.concatenate([qkv_share, vector_rows(vectors, 1, 3 * width)[0]], axis=0)
    first_gather = lax.all_gather(packed, "dp", axis=0)
    full_qkv = first_gather[:, :part].reshape(model, 3 * width)
    flat_vectors = first_gather[:, part:].reshape(shards, -1).astype(F32)

    def vector(index):
        return flat_vectors[:, index * part : (index + 1) * part].reshape(model)

    query_bias = lax.dynamic_slice_in_dim(vector(0), rank * width, width)
    value_bias = lax.dynamic_slice_in_dim(vector(1), rank * width, width)
    attn_bias = vector(2)
    gain_first, shift_first, gain_second, shift_second, proj_bias = (
        vector(3),
        vector(4),
        vector(5),
        vector(6),
        vector(7),
    )
    fc_bias = lax.dynamic_index_in_dim(
        flat_vectors[:, 8 * part : 8 * part + hidden_part].reshape(shards, ranks, units),
        rank,
        1,
        keepdims=False,
    ).reshape(hidden_width)

    fc_share = lax.dynamic_index_in_dim(
        w_fc.reshape(part, shards, ranks, units), rank, 2, keepdims=False
    ).reshape(part, hidden_width)
    proj_share = lax.dynamic_index_in_dim(
        w_proj.reshape(ranks, units, model), rank, 0, keepdims=False
    ).reshape(part, units * model // part)
    attn_share = lax.dynamic_slice_in_dim(w_attn, rank * width, width, 1)
    second_gather = lax.all_gather(
        jnp.concatenate([attn_share, fc_share, proj_share], axis=1), "dp", axis=0
    )
    attn_columns = second_gather[:, :, :width].reshape(model, width)
    share_fc = second_gather[:, :, width : width + hidden_width].reshape(model, hidden_width)
    share_proj = second_gather[:, :, width + hidden_width :].reshape(hidden_width, model)

    all_tokens = in_rank_order(gather_offsets(tokens)).transpose(1, 0, 2, 3)
    all_tokens = all_tokens.reshape(seqs * length, model)
    cot_blocks = gather_offsets(cot_own)

    unit_all, _ = row_stats(all_tokens.astype(F32))
    normed = (unit_all * gain_first + shift_first).astype(BF16)
    joint_bias = jnp.concatenate([query_bias, jnp.zeros_like(query_bias), value_bias])
    mixed = (dot_nn(normed, full_qkv) + joint_bias).astype(BF16)
    mixed = mixed.reshape(seqs, length, 3 * width)
    attended, logs = attend(mixed, width)

    sent = by_offset(attended.reshape(seqs, ranks, rows, width), 1)
    arrived = [sent[0]] + [swap(sent[offset], offset) for offset in range(1, ranks)]
    joined = in_rank_order(arrived).transpose(1, 2, 0, 3).reshape(seqs * rows, model)
    full_attn = in_rank_order(gather_offsets(attn_columns)).transpose(1, 0, 2)
    full_attn = full_attn.reshape(model, model)

    inputs = tokens_own.astype(F32)
    middle = inputs + (dot_nn(joined, full_attn) + attn_bias)
    unit_two, inverse_two = row_stats(middle)
    normed_two = (unit_two * gain_second + shift_second).astype(BF16)
    all_two = jnp.concatenate(gather_offsets(normed_two), axis=0)
    all_cot = jnp.concatenate(cot_blocks, axis=0)

    hidden = dot_nn(all_two, share_fc) + fc_bias
    active, gelu_pull = jax.vjp(gelu_tanh, hidden)
    active = active.astype(BF16)
    grad_active = dot_nt(all_cot, share_proj)
    grad_hidden = gelu_pull(grad_active)[0].astype(BF16)
    back_two = dot_nt(grad_hidden, share_fc).astype(BF16).reshape(ranks, seqs * rows, model)
    grad_normed_two = reduce_offsets([back_two[offset] for offset in range(ranks)])
    forward_two = dot_nn(active, share_proj).astype(BF16).reshape(ranks, seqs * rows, model)
    projected = reduce_offsets([forward_two[offset] for offset in range(ranks)])
    output = (middle + projected + proj_bias).astype(BF16)

    upstream = cot_own.astype(F32)
    grad_gain_two = jnp.sum(grad_normed_two * unit_two, axis=0)
    grad_shift_two = jnp.sum(grad_normed_two, axis=0)
    grad_middle = upstream + norm_back(grad_normed_two, gain_second, unit_two, inverse_two)
    grad_branch = grad_middle.astype(BF16)
    grad_joined = dot_nt(grad_branch, full_attn).astype(BF16)
    grad_sent = by_offset(grad_joined.reshape(seqs, rows, ranks, width), 2)
    grad_arrived = [grad_sent[0]] + [
        swap(grad_sent[offset], offset) for offset in range(1, ranks)
    ]
    grad_attended = in_rank_order(grad_arrived).transpose(1, 0, 2, 3)
    grad_attended = grad_attended.reshape(seqs, length, width)

    grad_w_proj = dot_tn(active, all_cot).astype(BF16).reshape(shards, units, model)
    grad_w_fc = dot_tn(all_two, grad_hidden).astype(BF16).reshape(shards, part, hidden_width)
    grad_bias_fc = jnp.sum(grad_hidden, axis=0, dtype=F32)
    grad_bias_proj = jnp.sum(upstream, axis=0)
    first_scatter = lax.psum_scatter(
        jnp.concatenate(
            [
                grad_w_fc,
                grad_w_proj.reshape(shards, part, units * model // part),
            ],
            axis=2,
        ),
        "dp",
        scatter_dimension=0,
    )

    grad_attn_part = dot_tn(joined, grad_branch).reshape(model, ranks, width)
    grad_w_attn = reduce_offsets(by_offset(grad_attn_part, 1)).astype(BF16)
    grad_bias_attn = jnp.sum(grad_branch, axis=0, dtype=F32)

    grad_mixed = attend_back(mixed, attended, grad_attended, logs, width)
    grad_mixed = grad_mixed.reshape(seqs * length, 3 * width)
    back_one = dot_nt(grad_mixed, full_qkv).astype(BF16)
    blocks_one = by_offset(back_one.reshape(seqs, ranks, rows, model), 1)
    grad_normed = reduce_offsets(blocks_one).reshape(seqs * rows, model)
    grad_w_qkv = dot_tn(normed, grad_mixed).astype(BF16)
    column_sums = jnp.sum(grad_mixed, axis=0, dtype=F32)
    grad_gain_one = jnp.sum(back_one.astype(F32) * unit_all, axis=0)
    grad_shift_one = jnp.sum(back_one, axis=0, dtype=F32)

    def spread(values):
        return lax.dynamic_update_slice_in_dim(
            jnp.zeros((model,), F32), values, rank * width, 0
        )

    grad_vectors = (
        spread(column_sums[:width]),
        spread(column_sums[2 * width :]),
        grad_bias_attn,
        grad_gain_one,
        grad_shift_one,
        grad_gain_two,
        grad_shift_two,
        grad_bias_proj,
        grad_bias_fc,
    )
    last_columns = 4 * width
    vector_part = vector_rows(grad_vectors, shards, last_columns).astype(BF16)
    last_scatter = lax.psum_scatter(
        jnp.concatenate(
            [
                jnp.concatenate(
                    [
                        grad_w_qkv.reshape(shards, part, 3 * width),
                        grad_w_attn.reshape(shards, part, width),
                    ],
                    axis=2,
                ),
                vector_part,
            ],
            axis=1,
        ),
        "dp",
        scatter_dimension=0,
    )

    unit_one, inverse_one = row_stats(inputs)
    grad_tokens = grad_middle + norm_back(grad_normed, gain_first, unit_one, inverse_one)

    feed = in_rank_order(gather_offsets(first_scatter))
    out_fc = feed[:, :, :hidden_width].reshape(ranks, part, shards, units)
    out_fc = out_fc.transpose(1, 2, 0, 3).reshape(part, w_fc.shape[1]).astype(F32)
    out_proj = feed[:, :, hidden_width:].reshape(hidden_part, model).astype(F32)
    rest = in_rank_order(gather_offsets(last_scatter))
    out_qkv = rest[:, :part, : 3 * width].reshape(ranks, part, 3, width)
    out_qkv = out_qkv.transpose(1, 2, 0, 3).reshape(part, 3 * model).astype(F32)
    out_attn = rest[:, :part, 3 * width :].transpose(1, 0, 2).reshape(part, model).astype(F32)
    out_vectors = rest[:, part:].reshape(ranks, -1).astype(F32)
    summed = jnp.sum(out_vectors[:, : 8 * part], axis=0)
    out_bias_fc = out_vectors[:, 8 * part : 8 * part + units].reshape(hidden_part)

    def out_vector(index):
        return summed[index * part : (index + 1) * part]

    return (
        output.reshape(seqs, rows, model),
        grad_tokens.reshape(seqs, rows, model),
        out_qkv,
        out_attn,
        out_fc,
        out_proj,
        out_vector(0),
        out_vector(1),
        out_vector(2),
        out_vector(3),
        out_vector(4),
        out_vector(5),
        out_vector(6),
        out_bias_fc,
        out_vector(7),
    )


def solution(mesh):
    token_spec = P("dp", "seq", None)
    in_specs = (token_spec,) * 2 + (P("dp", None),) * 4 + (P("dp"),) * 9
    out_specs = (token_spec,) * 2 + (P("dp", None),) * 4 + (P("dp"),) * 9
    return jax.shard_map(
        per_device, mesh=mesh, in_specs=in_specs, out_specs=out_specs, check_vma=False
    )
```

```python
import functools

import jax
import jax.numpy as jnp
from jax import lax
from jax.experimental import pallas as pl
from jax.experimental.pallas import tpu as pltpu
from jax.sharding import PartitionSpec as P

HEAD_DIM = 64
EPSILON = 1e-05
ROOT_COEF = 0.7978845608028654
SCALE = HEAD_DIM ** (-0.5)
BF16 = jnp.bfloat16
F32 = jnp.float32
LOG_ROWS = 8
VMEM_BYTES = 56 * 1024 * 1024


def gelu_tanh(values):
    return (
        0.5 * values * (1.0 + jnp.tanh(ROOT_COEF * (values + 0.044715 * values * values * values)))
    )


def dot_nn(left_side, right_side):
    return lax.dot_general(
        left_side, right_side, (((1,), (0,)), ((), ())), preferred_element_type=F32
    )


def dot_nt(left_side, right_side):
    return lax.dot_general(
        left_side, right_side, (((1,), (1,)), ((), ())), preferred_element_type=F32
    )


def dot_tn(left_side, right_side):
    return lax.dot_general(
        left_side, right_side, (((0,), (0,)), ((), ())), preferred_element_type=F32
    )


def head_lanes(array, head):
    lanes = lax.broadcasted_iota(jnp.int32, array.shape, 1)
    owner = lax.shift_right_logical(lanes, 6)
    return jnp.where(owner == head, array.astype(F32), 0.0)


def attend_kernel(mixed_ref, out_ref, log_ref, *, block, width):
    length = mixed_ref.shape[1]
    heads = width // HEAD_DIM
    step = 4 if heads % 4 == 0 else 1
    for index in range(length // block):
        first, stop = index * block, (index + 1) * block
        query = mixed_ref[0, first:stop, 0:width]
        row_pos = lax.broadcasted_iota(jnp.int32, (block, block), 0)
        col_pos = lax.broadcasted_iota(jnp.int32, (block, block), 1)
        allowed = row_pos >= col_pos
        log_lanes = lax.broadcasted_iota(jnp.int32, (block, 128), 1)

        def one_head(head, carry):
            total, logs = carry
            masked = (head_lanes(query, head) * SCALE).astype(BF16)
            diagonal = dot_nt(masked, mixed_ref[0, first:stop, width : 2 * width])
            diagonal = jnp.where(allowed, diagonal, -1e30)
            largest = jnp.max(diagonal, axis=1, keepdims=True)
            if first:
                scores = dot_nt(masked, mixed_ref[0, 0:first, width : 2 * width])
                largest = jnp.maximum(largest, jnp.max(scores, axis=1, keepdims=True))
            weights = jnp.exp(diagonal - largest)
            row_total = jnp.sum(weights, axis=1, keepdims=True)
            mixed = dot_nn(
                weights.astype(BF16), mixed_ref[0, first:stop, 2 * width : 3 * width]
            )
            if first:
                weights = jnp.exp(scores - largest)
                row_total = row_total + jnp.sum(weights, axis=1, keepdims=True)
                mixed = mixed + dot_nn(
                    weights.astype(BF16), mixed_ref[0, 0:first, 2 * width : 3 * width]
                )
            total = total + head_lanes(mixed * (1.0 / row_total), head)
            logs = jnp.where(log_lanes == head, largest + jnp.log(row_total), logs)
            return (total, logs)

        def some_heads(group, carry):
            for inner in range(step):
                carry = one_head(group * step + inner, carry)
            return carry

        total, logs = lax.fori_loop(
            0,
            heads // step,
            some_heads,
            (jnp.zeros((block, width), F32), jnp.zeros((block, 128), F32)),
        )
        out_ref[0, first:stop, :] = total.astype(BF16)
        log_ref[0, :, first:stop] = jnp.transpose(logs)[0:LOG_ROWS]


def attend(mixed, width):
    seqs, length, _ = mixed.shape
    block = min(256, length)
    return pl.pallas_call(
        functools.partial(attend_kernel, block=block, width=width),
        grid=(seqs,),
        in_specs=[pl.BlockSpec((1, length, 3 * width), lambda s: (s, 0, 0))],
        out_specs=[
            pl.BlockSpec((1, length, width), lambda s: (s, 0, 0)),
            pl.BlockSpec((1, LOG_ROWS, length), lambda s: (s, 0, 0)),
        ],
        out_shape=[
            jax.ShapeDtypeStruct((seqs, length, width), BF16),
            jax.ShapeDtypeStruct((seqs, LOG_ROWS, length), F32),
        ],
        compiler_params=pltpu.CompilerParams(vmem_limit_bytes=VMEM_BYTES),
        cost_estimate=pl.CostEstimate(
            flops=28 * seqs * length * length * width,
            bytes_accessed=8 * seqs * length * width,
            transcendentals=seqs * length * length * width // HEAD_DIM // 2,
        ),
    )(mixed)


def attend_back_kernel(
    mixed_ref,
    out_ref,
    grad_ref,
    log_ref,
    result_ref,
    query_heads,
    key_heads,
    grad_heads,
    grad_query,
    grad_key,
    grad_value,
    inner_rows,
    *,
    block,
    width,
):
    length = mixed_ref.shape[1]
    heads = width // HEAD_DIM
    blocks = length // block
    owner = lax.shift_right_logical(lax.broadcasted_iota(jnp.int32, (LOG_ROWS, width), 1), 6)
    picks = (owner == lax.broadcasted_iota(jnp.int32, (LOG_ROWS, width), 0)).astype(F32)

    def prepare(index, carry):
        rows = pl.ds(pl.multiple_of(index * block, block), block)
        query = mixed_ref[0, rows, 0:width]
        key = mixed_ref[0, rows, width : 2 * width]
        grad = grad_ref[0, rows, :]
        for head in range(heads):
            query_heads[head, rows, :] = (head_lanes(query, head) * SCALE).astype(BF16)
            key_heads[head, rows, :] = head_lanes(key, head).astype(BF16)
            grad_heads[head, rows, :] = head_lanes(grad, head).astype(BF16)
        product = grad.astype(F32) * out_ref[0, rows, :].astype(F32)
        inner_rows[:, rows] = lax.dot_general(
            picks,
            product,
            (((1,), (1,)), ((), ())),
            precision=lax.Precision.HIGHEST,
            preferred_element_type=F32,
        )
        zeros = jnp.zeros((block, width), F32)
        grad_query[rows, :] = zeros
        grad_key[rows, :] = zeros
        grad_value[rows, :] = zeros
        return carry

    lax.fori_loop(0, blocks, prepare, 0)

    def tile(row_block, col_block, on_diagonal):
        rows = pl.ds(pl.multiple_of(row_block * block, block), block)
        cols = pl.ds(pl.multiple_of(col_block * block, block), block)
        key = mixed_ref[0, cols, width : 2 * width]
        value = mixed_ref[0, cols, 2 * width : 3 * width]
        add_query = add_key = add_value = None
        for head in range(heads):
            query = query_heads[head, rows, :]
            grad = grad_heads[head, rows, :]
            probs = jnp.exp(dot_nt(key, query) - log_ref[0, head : head + 1, rows])
            if on_diagonal:
                key_pos = lax.broadcasted_iota(jnp.int32, (block, block), 0)
                row_pos = lax.broadcasted_iota(jnp.int32, (block, block), 1)
                probs = jnp.where(row_pos >= key_pos, probs, 0.0)
            grad_probs = dot_nt(value, grad)
            grad_scores = (probs * (grad_probs - inner_rows[head : head + 1, rows])).astype(BF16)
            one_value = dot_nn(probs.astype(BF16), grad)
            one_key = dot_nn(grad_scores, query)
            one_query = dot_tn(grad_scores, key_heads[head, cols, :])
            add_value = one_value if head == 0 else add_value + one_value
            add_key = one_key if head == 0 else add_key + one_key
            add_query = one_query if head == 0 else add_query + one_query
        grad_value[cols, :] += add_value
        grad_key[cols, :] += add_key
        grad_query[rows, :] += add_query

    def row_step(row_block, carry):
        def col_step(col_block, inner_carry):
            tile(row_block, col_block, False)
            return inner_carry

        lax.fori_loop(0, row_block, col_step, 0)
        tile(row_block, row_block, True)
        return carry

    lax.fori_loop(0, blocks, row_step, 0)

    def finish(index, carry):
        rows = pl.ds(pl.multiple_of(index * block, block), block)
        result_ref[0, rows, 0:width] = (grad_query[rows, :] * SCALE).astype(BF16)
        result_ref[0, rows, width : 2 * width] = grad_key[rows, :].astype(BF16)
        result_ref[0, rows, 2 * width : 3 * width] = grad_value[rows, :].astype(BF16)
        return carry

    lax.fori_loop(0, blocks, finish, 0)


def attend_back(mixed, attended, grad_attended, logs, width):
    seqs, length, _ = mixed.shape
    heads = width // HEAD_DIM
    block = min(512, length)
    return pl.pallas_call(
        functools.partial(attend_back_kernel, block=block, width=width),
        grid=(seqs,),
        in_specs=[
            pl.BlockSpec((1, length, 3 * width), lambda s: (s, 0, 0)),
            pl.BlockSpec((1, length, width), lambda s: (s, 0, 0)),
            pl.BlockSpec((1, length, width), lambda s: (s, 0, 0)),
            pl.BlockSpec((1, LOG_ROWS, length), lambda s: (s, 0, 0)),
        ],
        out_specs=pl.BlockSpec((1, length, 3 * width), lambda s: (s, 0, 0)),
        out_shape=jax.ShapeDtypeStruct((seqs, length, 3 * width), BF16),
        scratch_shapes=[
            pltpu.VMEM((heads, length, width), BF16),
            pltpu.VMEM((heads, length, width), BF16),
            pltpu.VMEM((heads, length, width), BF16),
            pltpu.VMEM((length, width), F32),
            pltpu.VMEM((length, width), F32),
            pltpu.VMEM((length, width), F32),
            pltpu.VMEM((LOG_ROWS, length), F32),
        ],
        compiler_params=pltpu.CompilerParams(vmem_limit_bytes=VMEM_BYTES),
        cost_estimate=pl.CostEstimate(
            flops=56 * seqs * length * length * width,
            bytes_accessed=16 * seqs * length * width,
            transcendentals=seqs * length * length * width // HEAD_DIM // 2,
        ),
    )(mixed, attended, grad_attended, logs)


def feed_kernel(
    normed_ref,
    cot_ref,
    fc_ref,
    proj_ref,
    bias_ref,
    active_ref,
    grad_ref,
    back_ref,
    ahead_ref,
    sum_ref,
):
    hidden = dot_nn(normed_ref[...], fc_ref[...]) + bias_ref[...]
    grad_active = dot_nt(cot_ref[...], proj_ref[...])
    square = hidden * hidden
    curve = jnp.tanh(ROOT_COEF * hidden * (1.0 + 0.044715 * square))
    half = 0.5 + 0.5 * curve
    active = (hidden * half).astype(BF16)
    slope = half + hidden * (0.5 - 0.5 * curve * curve) * (
        ROOT_COEF + (3.0 * 0.044715 * ROOT_COEF) * square
    )
    grad = (grad_active * slope).astype(BF16)
    active_ref[...] = active
    grad_ref[...] = grad
    back_ref[...] = dot_nt(grad, fc_ref[...]).astype(BF16)
    ahead_ref[...] = dot_nn(active, proj_ref[...]).astype(BF16)
    sums = jnp.sum(grad.astype(F32), axis=0, keepdims=True)

    @pl.when(pl.program_id(0) == 0)
    def _():
        sum_ref[...] = jnp.zeros_like(sum_ref)

    sum_ref[...] += sums


def feed(normed, cotangent, share_fc, share_proj, bias):
    rows, model = normed.shape
    width = share_fc.shape[1]
    block = min(256, rows)
    row_spec = pl.BlockSpec((block, model), lambda i: (i, 0))
    wide_spec = pl.BlockSpec((block, width), lambda i: (i, 0))
    return pl.pallas_call(
        feed_kernel,
        grid=(rows // block,),
        in_specs=[
            row_spec,
            row_spec,
            pl.BlockSpec((model, width), lambda i: (0, 0)),
            pl.BlockSpec((width, model), lambda i: (0, 0)),
            pl.BlockSpec((1, width), lambda i: (0, 0)),
        ],
        out_specs=[
            wide_spec,
            wide_spec,
            row_spec,
            row_spec,
            pl.BlockSpec((1, width), lambda i: (0, 0)),
        ],
        out_shape=[
            jax.ShapeDtypeStruct((rows, width), BF16),
            jax.ShapeDtypeStruct((rows, width), BF16),
            jax.ShapeDtypeStruct((rows, model), BF16),
            jax.ShapeDtypeStruct((rows, model), BF16),
            jax.ShapeDtypeStruct((1, width), F32),
        ],
        compiler_params=pltpu.CompilerParams(vmem_limit_bytes=VMEM_BYTES),
        cost_estimate=pl.CostEstimate(
            flops=14 * rows * model * width,
            bytes_accessed=8 * rows * model + 4 * rows * width + 4 * model * width,
            transcendentals=rows * width,
        ),
    )(normed, cotangent, share_fc, share_proj, bias)


def ring_order(shards):
    fast = 1
    while fast * fast * 4 <= shards:
        fast *= 2
    slow = shards // fast
    if fast == 1:
        return list(range(shards))
    path = [row * fast for row in range(slow)]
    for row in reversed(range(slow)):
        line = range(1, fast) if (slow - 1 - row) % 2 == 0 else reversed(range(1, fast))
        path += [row * fast + place for place in line]
    return path


def ring_move(array, towards):
    order = ring_order(lax.axis_size("dp"))
    shards = len(order)
    pairs = [(order[i], order[(i + towards) % shards]) for i in range(shards)]
    return lax.ppermute(array, "dp", pairs)


def ring_lookup(distance):
    order = ring_order(lax.axis_size("dp"))
    shards = len(order)
    table = [0] * shards
    for place, device in enumerate(order):
        table[device] = order[(place + distance) % shards]
    return jnp.array(table, jnp.int32)[lax.axis_index("dp")]


def ring_gather(share, ties):
    shards = lax.axis_size("dp")
    full = jnp.zeros((shards,) + share.shape, share.dtype)
    full = lax.dynamic_update_index_in_dim(full, share, lax.axis_index("dp"), 0)
    upward = downward = share
    tied = {}
    for step in range(1, shards // 2 + 1):
        upward = ring_move(upward, 1)
        if 2 * step < shards:
            downward = ring_move(downward, -1)
        full = lax.dynamic_update_index_in_dim(full, upward, ring_lookup(-step), 0)
        if 2 * step < shards:
            full = lax.dynamic_update_index_in_dim(full, downward, ring_lookup(step), 0)
        if step in ties:
            upward, tied[step] = lax.optimization_barrier((upward, ties[step]))
    return full, tied


def ring_scatter(parts, tie):
    shards = parts.shape[0]
    half = shards // 2

    def own(distance):
        return lax.dynamic_index_in_dim(parts, ring_lookup(distance), 0, keepdims=False)

    downward = upward = None
    for distance in range(half, 0, -1):
        held = own(-distance)
        if downward is not None:
            held = (held.astype(F32) + downward.astype(F32)).astype(BF16)
        if distance == 1:
            held, tie = lax.optimization_barrier((held, tie))
        downward = ring_move(held, -1)
        if distance < half or 2 * half < shards:
            held = own(distance)
            if upward is not None:
                held = (held.astype(F32) + upward.astype(F32)).astype(BF16)
            upward = ring_move(held, 1)
    total = own(0).astype(F32) + downward.astype(F32)
    return (total if upward is None else total + upward.astype(F32)), tie


def swap(array, offset):
    ranks = lax.axis_size("seq")
    return lax.ppermute(array, "seq", [(rank, rank ^ offset) for rank in range(ranks)])


def bits_up():
    ranks, bits, bit = (lax.axis_size("seq"), [], 1)
    while bit < ranks:
        bits.append(bit)
        bit *= 2
    return bits


def gather_offsets(array, bits=None):
    found = {0: array}
    for bit in reversed(bits_up() if bits is None else bits):
        for offset in sorted(found):
            found[offset | bit] = swap(found[offset], bit)
    return [found[offset] for offset in range(len(found))]


def reduce_offsets(blocks, bits=None):
    left = dict(enumerate(blocks))
    for bit in bits_up() if bits is None else bits:
        for offset in sorted(left, reverse=True):
            if offset & bit:
                arrived = swap(left.pop(offset).astype(BF16), bit)
                left[offset ^ bit] = left[offset ^ bit].astype(F32) + arrived.astype(F32)
    return left[0]


def placed(blocks, axis):
    rank = lax.axis_index("seq")
    size = blocks[0].shape[axis]
    shape = list(blocks[0].shape)
    shape[axis] = size * len(blocks)
    full = jnp.zeros(shape, blocks[0].dtype)
    for offset, block in enumerate(blocks):
        full = lax.dynamic_update_slice_in_dim(full, block, (rank ^ offset) * size, axis)
    return full


def picked(array, axis):
    rank, ranks = (lax.axis_index("seq"), lax.axis_size("seq"))
    size = array.shape[axis] // ranks
    return [
        lax.dynamic_slice_in_dim(array, (rank ^ offset) * size, size, axis)
        for offset in range(ranks)
    ]


def columns_kernel(rank_ref, *refs, groups, size):
    blocks, full_ref = (refs[:-1], refs[-1])
    ranks = len(blocks)
    for offset, block_ref in enumerate(blocks):
        owner = lax.bitwise_xor(rank_ref[0, 0], offset)
        for group in range(groups):
            start = pl.multiple_of((owner + group * ranks) * size, size)
            piece = block_ref[:, group * size : (group + 1) * size]
            full_ref[:, pl.ds(start, size)] = piece.astype(full_ref.dtype)


def columns(blocks, groups, dtype):
    rows, wide = blocks[0].shape
    ranks, size = (len(blocks), wide // groups)
    rank = lax.axis_index("seq")
    if size % 128:
        shaped = [block.reshape(rows, groups, 1, size) for block in blocks]
        return placed(shaped, 2).reshape(rows, ranks * wide).astype(dtype)
    return pl.pallas_call(
        functools.partial(columns_kernel, groups=groups, size=size),
        in_specs=[pl.BlockSpec(memory_space=pltpu.SMEM)]
        + [pl.BlockSpec(memory_space=pltpu.VMEM)] * ranks,
        out_specs=pl.BlockSpec(memory_space=pltpu.VMEM),
        out_shape=jax.ShapeDtypeStruct((rows, ranks * wide), dtype),
        compiler_params=pltpu.CompilerParams(vmem_limit_bytes=VMEM_BYTES),
        cost_estimate=pl.CostEstimate(
            flops=rows * wide * ranks, bytes_accessed=6 * rows * wide * ranks, transcendentals=0
        ),
    )(rank.astype(jnp.int32).reshape(1, 1), *blocks)


def row_stats(values):
    average = jnp.mean(values, axis=-1, keepdims=True)
    centered = values - average
    variance = jnp.mean(centered * centered, axis=-1, keepdims=True)
    inverse = lax.rsqrt(variance + EPSILON)
    return centered * inverse, inverse


def norm_back(incoming, gain, unit, inverse):
    scaled = incoming * gain
    first = jnp.mean(scaled, axis=-1, keepdims=True)
    second = jnp.mean(scaled * unit, axis=-1, keepdims=True)
    return inverse * (scaled - first - unit * second)


def vector_rows(vectors, columns_count):
    padded = [
        jnp.pad(item, ((0, 0), (0, columns_count - item.shape[1])))[:, None] for item in vectors
    ]
    stacked = jnp.concatenate(padded, axis=1)
    return jnp.pad(stacked, ((0, 0), (0, -stacked.shape[1] % 16), (0, 0)))


def per_device(
    tokens,
    cotangent,
    w_qkv,
    w_attn,
    w_fc,
    w_proj,
    bias_query,
    bias_value,
    bias_attn,
    gain_one,
    shift_one,
    gain_two,
    shift_two,
    bias_fc,
    bias_proj,
):
    ranks = lax.axis_size("seq")
    shards = lax.axis_size("dp")
    rank = lax.axis_index("seq")
    seqs, rows, model = tokens.shape
    length = rows * ranks
    width = model // ranks
    part = w_qkv.shape[0]
    hidden_part = w_proj.shape[0]
    units = hidden_part // ranks
    hidden_width = w_fc.shape[1] // ranks
    tokens_own = tokens.reshape(seqs * rows, model)
    cot_own = cotangent.reshape(seqs * rows, model)
    gather_columns = 4 * width

    def share_of(array, groups):
        size = array.shape[1] // (groups * ranks)
        return [
            lax.dynamic_slice_in_dim(array, (group * ranks + rank) * size, size, 1)
            for group in range(groups)
        ]

    vectors = [
        item.reshape(1, part)
        for item in (
            bias_query,
            bias_value,
            bias_attn,
            gain_one,
            shift_one,
            gain_two,
            shift_two,
            bias_proj,
        )
    ] + [item.reshape(1, units) for item in jnp.split(bias_fc, ranks)]
    packed = jnp.concatenate(
        [
            jnp.concatenate(share_of(w_qkv, 3) + share_of(w_attn, 1), axis=1),
            vector_rows(vectors, gather_columns)[0],
        ],
        axis=0,
    )
    proj_share = lax.dynamic_slice_in_dim(w_proj, rank * units, units, 0)
    feed_share = jnp.concatenate(
        share_of(w_fc, shards) + [proj_share.reshape(part, units * model // part)], axis=1
    )

    all_tokens = placed(gather_offsets(tokens), 1).reshape(seqs * length, model)
    token_values = all_tokens.astype(F32)
    average = jnp.mean(token_values, axis=-1, keepdims=True)
    centered = token_values - average
    inverse_all = lax.rsqrt(jnp.mean(centered * centered, axis=-1, keepdims=True) + EPSILON)

    steps = shards // 2
    middle_step = max(1, steps // 2)
    first_gather, tied = ring_gather(
        packed,
        {middle_step: (feed_share,), steps - 1: (average, inverse_all, all_tokens)},
    )
    (feed_share,) = tied[middle_step]
    average, inverse_all, all_tokens = tied[steps - 1]
    second_gather = lax.all_gather(feed_share, "dp", axis=0)
    share_fc = second_gather[:, :, :hidden_width].reshape(model, hidden_width)
    share_proj = second_gather[:, :, hidden_width:].reshape(hidden_width, model)
    full_qkv = first_gather[:, :part, : 3 * width].reshape(model, 3 * width)
    attn_columns = first_gather[:, :part, 3 * width :].reshape(model, width)
    vector_block = first_gather[:, part:].astype(F32)

    def vector(index):
        return vector_block[:, index, :part].reshape(model)

    query_bias = lax.dynamic_slice_in_dim(vector(0), rank * width, width)
    value_bias = lax.dynamic_slice_in_dim(vector(1), rank * width, width)
    attn_bias = vector(2)
    gain_first, shift_first, gain_second, shift_second, proj_bias = (
        vector(3),
        vector(4),
        vector(5),
        vector(6),
        vector(7),
    )
    fc_bias = lax.dynamic_index_in_dim(vector_block, 8 + rank, 1, keepdims=False)
    fc_bias = fc_bias[:, :units].reshape(hidden_width)
    cot_blocks = gather_offsets(cot_own)
    half = ranks // 2
    near_cot = jnp.concatenate(cot_blocks[:half], axis=0)
    far_cot = jnp.concatenate(cot_blocks[half:], axis=0)

    unit_all = (all_tokens.astype(F32) - average) * inverse_all
    normed = (unit_all * gain_first + shift_first).astype(BF16)
    joint_bias = jnp.concatenate([query_bias, jnp.zeros_like(query_bias), value_bias])
    mixed = (dot_nn(normed, full_qkv) + joint_bias).astype(BF16)
    mixed = mixed.reshape(seqs, length, 3 * width)
    mixed, near_cot, far_cot = lax.optimization_barrier((mixed, near_cot, far_cot))
    attended, logs = attend(mixed, width)

    sent = picked(attended, 1)
    arrived = [sent[0]] + [swap(sent[offset], offset) for offset in range(1, ranks)]
    joined = columns([item.reshape(seqs * rows, width) for item in arrived], 1, BF16)
    full_attn = columns(gather_offsets(attn_columns), 1, BF16)

    inputs = tokens_own.astype(F32)
    middle = inputs + (dot_nn(joined, full_attn) + attn_bias)
    unit_two, inverse_two = row_stats(middle)
    normed_two = (unit_two * gain_second + shift_second).astype(BF16)
    *low_bits, top_bit = bits_up()
    near_two = jnp.concatenate(gather_offsets(normed_two, low_bits), axis=0)
    far_two = jnp.concatenate(gather_offsets(swap(normed_two, top_bit), low_bits), axis=0)
    feed_bias = fc_bias.reshape(1, hidden_width)
    near_active, near_grad, near_back, near_ahead, near_sum = feed(
        near_two, near_cot, share_fc, share_proj, feed_bias
    )
    far_active, far_grad, far_back, far_ahead, far_sum = feed(
        far_two, far_cot, share_fc, share_proj, feed_bias
    )

    def reduce_halves(near, far):
        blocks = (half, seqs * rows, model)
        far_part = reduce_offsets(list(far.reshape(blocks)), low_bits).astype(BF16)
        near_part = reduce_offsets(list(near.reshape(blocks)), low_bits)
        return near_part.astype(F32), swap(far_part, top_bit)

    near_part, far_part = reduce_halves(near_back, far_back)
    grad_normed_two = near_part + far_part.astype(F32)

    upstream = cot_own.astype(F32)
    grad_gain_two = jnp.sum(grad_normed_two * unit_two, axis=0)
    grad_shift_two = jnp.sum(grad_normed_two, axis=0)
    grad_middle = upstream + norm_back(grad_normed_two, gain_second, unit_two, inverse_two)
    grad_branch = grad_middle.astype(BF16)
    grad_joined = dot_nt(grad_branch, full_attn).astype(BF16)
    grad_sent = picked(grad_joined.reshape(seqs, rows, model), 2)
    grad_arrived = [grad_sent[0]] + [
        swap(grad_sent[offset], offset) for offset in range(1, ranks)
    ]
    grad_attended = placed(grad_arrived, 1)

    grad_w_proj = dot_tn(near_active, near_cot) + dot_tn(far_active, far_cot)
    grad_w_proj = grad_w_proj.astype(BF16).reshape(shards, part, units * model // part)
    grad_w_fc = dot_tn(near_two, near_grad) + dot_tn(far_two, far_grad)
    grad_w_fc = grad_w_fc.astype(BF16).reshape(shards, part, hidden_width)
    grad_bias_fc = (near_sum + far_sum).reshape(hidden_width)
    grad_bias_proj = jnp.sum(upstream, axis=0)
    first_parts = jnp.concatenate([grad_w_fc, grad_w_proj], axis=2)
    near_ahead, far_ahead, _ = lax.optimization_barrier((near_ahead, far_ahead, grad_branch))
    ahead_far = reduce_offsets(
        list(far_ahead.reshape(half, seqs * rows, model)), low_bits
    ).astype(BF16)
    grad_attn_part = dot_tn(joined, grad_branch).astype(BF16)
    grad_attended, first_parts, ahead_far, grad_attn_part = lax.optimization_barrier(
        (grad_attended, first_parts, ahead_far, grad_attn_part)
    )
    first_scatter = lax.psum_scatter(first_parts, "dp", scatter_dimension=0)
    ahead_far = swap(ahead_far, top_bit)
    ahead_part = reduce_offsets(list(near_ahead.reshape(half, seqs * rows, model)), low_bits)
    grad_w_attn = reduce_offsets(picked(grad_attn_part, 1)).astype(BF16)
    grad_bias_attn = jnp.sum(grad_branch, axis=0, dtype=F32)

    grad_mixed = attend_back(mixed, attended, grad_attended, logs, width)
    grad_mixed = grad_mixed.reshape(seqs * length, 3 * width)
    grad_w_qkv = dot_tn(normed, grad_mixed)
    column_sums = jnp.sum(grad_mixed, axis=0, dtype=F32)
    qkv_values = full_qkv.astype(F32)
    grad_shift_one = jnp.sum(qkv_values * column_sums, axis=1)
    grad_gain_one = (
        jnp.sum(qkv_values * grad_w_qkv, axis=1) - shift_first * grad_shift_one
    ) / gain_first

    def spread(values):
        return lax.dynamic_update_slice_in_dim(
            jnp.zeros((model,), F32), values, rank * width, 0
        )

    grad_vectors = [
        item.reshape(shards, -1).astype(BF16)
        for item in (
            spread(column_sums[:width]),
            spread(column_sums[2 * width :]),
            grad_bias_attn,
            grad_gain_one,
            grad_shift_one,
            grad_gain_two,
            grad_shift_two,
            grad_bias_proj,
            grad_bias_fc,
        )
    ]
    last_parts = jnp.concatenate(
        [
            jnp.concatenate(
                [
                    grad_w_qkv.astype(BF16).reshape(shards, part, 3 * width),
                    grad_w_attn.reshape(shards, part, width),
                ],
                axis=2,
            ),
            vector_rows(grad_vectors, gather_columns),
        ],
        axis=1,
    )
    back_one = dot_nt(grad_mixed, full_qkv).astype(BF16)
    blocks_one = [
        item.reshape(seqs * rows, model) for item in picked(back_one.reshape(seqs, length, model), 1)
    ]
    grad_normed = reduce_offsets(blocks_one)
    fed = gather_offsets(first_scatter)
    last_scatter, fed = ring_scatter(last_parts, fed)
    rest = gather_offsets(last_scatter.astype(BF16))

    _, ahead_far = lax.optimization_barrier((grad_mixed, ahead_far))
    output = (middle + ahead_part.astype(F32) + ahead_far.astype(F32) + proj_bias).astype(BF16)
    unit_one, inverse_one = row_stats(inputs)
    grad_tokens = grad_middle + norm_back(grad_normed, gain_first, unit_one, inverse_one)

    out_fc = columns([item[:, :hidden_width] for item in fed], shards, F32)
    proj_blocks = [item[:, hidden_width:].reshape(units, model) for item in fed]
    out_proj = placed(proj_blocks, 0).astype(F32)
    out_qkv = columns([item[:part, : 3 * width] for item in rest], 3, F32)
    out_attn = columns([item[:part, 3 * width :] for item in rest], 1, F32)
    tails = [item[part:].astype(F32) for item in rest]
    summed = sum(tails)[:, :part]
    out_bias_fc = placed([item[8, :units] for item in tails], 0)

    def out_vector(index):
        return summed[index]

    return (
        output.reshape(seqs, rows, model),
        grad_tokens.reshape(seqs, rows, model),
        out_qkv,
        out_attn,
        out_fc,
        out_proj,
        out_vector(0),
        out_vector(1),
        out_vector(2),
        out_vector(3),
        out_vector(4),
        out_vector(5),
        out_vector(6),
        out_bias_fc,
        out_vector(7),
    )


def solution(mesh):
    token_spec = P("dp", "seq", None)
    in_specs = (token_spec,) * 2 + (P("dp", None),) * 4 + (P("dp"),) * 9
    out_specs = (token_spec,) * 2 + (P("dp", None),) * 4 + (P("dp"),) * 9
    return jax.shard_map(
        per_device, mesh=mesh, in_specs=in_specs, out_specs=out_specs, check_vma=False
    )
```

```python
import functools

import jax
import jax.numpy as jnp
from jax import lax
from jax.experimental import pallas as pl
from jax.experimental.pallas import tpu as pltpu
from jax.sharding import PartitionSpec as P

HEAD_DIM = 64
EPSILON = 1e-05
ROOT_COEF = 0.7978845608028654
SCALE = HEAD_DIM ** (-0.5)
BF16 = jnp.bfloat16
F32 = jnp.float32
LOG_ROWS = 8
VMEM_BYTES = 56 * 1024 * 1024


def gelu_tanh(values):
    return (
        0.5 * values * (1.0 + jnp.tanh(ROOT_COEF * (values + 0.044715 * values * values * values)))
    )


def dot_nn(left_side, right_side):
    return lax.dot_general(
        left_side, right_side, (((1,), (0,)), ((), ())), preferred_element_type=F32
    )


def dot_nt(left_side, right_side):
    return lax.dot_general(
        left_side, right_side, (((1,), (1,)), ((), ())), preferred_element_type=F32
    )


def dot_tn(left_side, right_side):
    return lax.dot_general(
        left_side, right_side, (((0,), (0,)), ((), ())), preferred_element_type=F32
    )


def project_kernel(rank_ref, *refs, parts):
    del rank_ref
    block_refs = refs[:parts]
    weight_ref, gain_ref, shift_ref, bias_ref, normed_ref, mixed_ref = refs[parts:]
    place = pl.program_id(0)
    values = block_refs[0][0]
    for part in range(1, parts):
        values = jnp.where(place == part, block_refs[part][0], values)
    values = values.astype(F32)
    centered = values - jnp.mean(values, axis=-1, keepdims=True)
    inverse = lax.rsqrt(jnp.mean(centered * centered, axis=-1, keepdims=True) + EPSILON)
    normed = (centered * inverse * gain_ref[...] + shift_ref[...]).astype(BF16)
    normed_ref[0, 0] = normed
    mixed_ref[0, 0] = (dot_nn(normed, weight_ref[...]) + bias_ref[...]).astype(BF16)


def project(blocks, weight, gain, shift, bias):
    seqs, rows, model = blocks[0].shape
    parts, wide = (len(blocks), weight.shape[1])
    block = min(256, rows)
    steps = rows // block

    def block_spec(part):
        def index_map(p, s, b, rank_ref):
            seq = jnp.where(p < part, 0, jnp.where(p > part, seqs - 1, s))
            row = jnp.where(p < part, 0, jnp.where(p > part, steps - 1, b))
            return (seq, row, 0)

        return pl.BlockSpec((1, block, model), index_map)

    def whole_spec(*shape):
        return pl.BlockSpec(shape, lambda p, s, b, rank_ref: (0, 0))

    def out_spec(columns_count):
        return pl.BlockSpec(
            (1, 1, block, columns_count),
            lambda p, s, b, rank_ref: (s, lax.bitwise_xor(rank_ref[0], p), b, 0),
        )

    return pl.pallas_call(
        functools.partial(project_kernel, parts=parts),
        grid_spec=pltpu.PrefetchScalarGridSpec(
            num_scalar_prefetch=1,
            grid=(parts, seqs, steps),
            in_specs=[block_spec(part) for part in range(parts)]
            + [
                whole_spec(model, wide),
                whole_spec(1, model),
                whole_spec(1, model),
                whole_spec(1, wide),
            ],
            out_specs=[out_spec(model), out_spec(wide)],
        ),
        out_shape=[
            jax.ShapeDtypeStruct((seqs, parts, rows, model), BF16),
            jax.ShapeDtypeStruct((seqs, parts, rows, wide), BF16),
        ],
        compiler_params=pltpu.CompilerParams(vmem_limit_bytes=VMEM_BYTES),
        cost_estimate=pl.CostEstimate(
            flops=4 * parts * seqs * rows * model * wide,
            bytes_accessed=parts * seqs * rows * (4 * model + 2 * wide) + 2 * model * wide,
            transcendentals=parts * seqs * rows,
        ),
    )(
        lax.axis_index("seq").astype(jnp.int32).reshape(1),
        *blocks,
        weight,
        gain.reshape(1, model),
        shift.reshape(1, model),
        bias.reshape(1, wide),
    )


def head_lanes(array, head):
    lanes = lax.broadcasted_iota(jnp.int32, array.shape, 1)
    owner = lax.shift_right_logical(lanes, 6)
    return jnp.where(owner == head, array.astype(F32), 0.0)


def attend_kernel(mixed_ref, out_ref, log_ref, *, block, width):
    length = mixed_ref.shape[1]
    heads = width // HEAD_DIM
    step = 4 if heads % 4 == 0 else 1
    for index in range(length // block):
        first, stop = index * block, (index + 1) * block
        query = mixed_ref[0, first:stop, 0:width]
        row_pos = lax.broadcasted_iota(jnp.int32, (block, block), 0)
        col_pos = lax.broadcasted_iota(jnp.int32, (block, block), 1)
        allowed = row_pos >= col_pos
        log_lanes = lax.broadcasted_iota(jnp.int32, (block, 128), 1)

        def one_head(head, carry):
            total, logs = carry
            masked = (head_lanes(query, head) * SCALE).astype(BF16)
            diagonal = dot_nt(masked, mixed_ref[0, first:stop, width : 2 * width])
            diagonal = jnp.where(allowed, diagonal, -1e30)
            largest = jnp.max(diagonal, axis=1, keepdims=True)
            if first:
                scores = dot_nt(masked, mixed_ref[0, 0:first, width : 2 * width])
                largest = jnp.maximum(largest, jnp.max(scores, axis=1, keepdims=True))
            weights = jnp.exp(diagonal - largest)
            row_total = jnp.sum(weights, axis=1, keepdims=True)
            mixed = dot_nn(
                weights.astype(BF16), mixed_ref[0, first:stop, 2 * width : 3 * width]
            )
            if first:
                weights = jnp.exp(scores - largest)
                row_total = row_total + jnp.sum(weights, axis=1, keepdims=True)
                mixed = mixed + dot_nn(
                    weights.astype(BF16), mixed_ref[0, 0:first, 2 * width : 3 * width]
                )
            total = total + head_lanes(mixed * (1.0 / row_total), head)
            logs = jnp.where(log_lanes == head, largest + jnp.log(row_total), logs)
            return (total, logs)

        def some_heads(group, carry):
            for inner in range(step):
                carry = one_head(group * step + inner, carry)
            return carry

        total, logs = lax.fori_loop(
            0,
            heads // step,
            some_heads,
            (jnp.zeros((block, width), F32), jnp.zeros((block, 128), F32)),
        )
        out_ref[0, first:stop, :] = total.astype(BF16)
        log_ref[0, :, first:stop] = jnp.transpose(logs)[0:LOG_ROWS]


def attend(mixed, width):
    seqs, length, _ = mixed.shape
    block = min(256, length)
    return pl.pallas_call(
        functools.partial(attend_kernel, block=block, width=width),
        grid=(seqs,),
        in_specs=[pl.BlockSpec((1, length, 3 * width), lambda s: (s, 0, 0))],
        out_specs=[
            pl.BlockSpec((1, length, width), lambda s: (s, 0, 0)),
            pl.BlockSpec((1, LOG_ROWS, length), lambda s: (s, 0, 0)),
        ],
        out_shape=[
            jax.ShapeDtypeStruct((seqs, length, width), BF16),
            jax.ShapeDtypeStruct((seqs, LOG_ROWS, length), F32),
        ],
        compiler_params=pltpu.CompilerParams(vmem_limit_bytes=VMEM_BYTES),
        cost_estimate=pl.CostEstimate(
            flops=28 * seqs * length * length * width,
            bytes_accessed=8 * seqs * length * width,
            transcendentals=seqs * length * length * width // HEAD_DIM // 2,
        ),
    )(mixed)


def attend_back_kernel(
    mixed_ref,
    out_ref,
    grad_ref,
    log_ref,
    result_ref,
    sum_ref,
    query_heads,
    key_heads,
    grad_heads,
    grad_query,
    grad_key,
    grad_value,
    inner_rows,
    *,
    block,
    width,
):
    length = mixed_ref.shape[1]
    heads = width // HEAD_DIM
    blocks = length // block
    owner = lax.shift_right_logical(lax.broadcasted_iota(jnp.int32, (LOG_ROWS, width), 1), 6)
    picks = (owner == lax.broadcasted_iota(jnp.int32, (LOG_ROWS, width), 0)).astype(F32)

    def prepare(index, carry):
        rows = pl.ds(pl.multiple_of(index * block, block), block)
        query = mixed_ref[0, rows, 0:width]
        key = mixed_ref[0, rows, width : 2 * width]
        grad = grad_ref[0, rows, :]
        for head in range(heads):
            query_heads[head, rows, :] = (head_lanes(query, head) * SCALE).astype(BF16)
            key_heads[head, rows, :] = head_lanes(key, head).astype(BF16)
            grad_heads[head, rows, :] = head_lanes(grad, head).astype(BF16)
        product = grad.astype(F32) * out_ref[0, rows, :].astype(F32)
        inner_rows[:, rows] = lax.dot_general(
            picks,
            product,
            (((1,), (1,)), ((), ())),
            precision=lax.Precision.HIGHEST,
            preferred_element_type=F32,
        )
        zeros = jnp.zeros((block, width), F32)
        grad_query[rows, :] = zeros
        grad_key[rows, :] = zeros
        grad_value[rows, :] = zeros
        return carry

    lax.fori_loop(0, blocks, prepare, 0)

    def tile(row_block, col_block, on_diagonal):
        rows = pl.ds(pl.multiple_of(row_block * block, block), block)
        cols = pl.ds(pl.multiple_of(col_block * block, block), block)
        key = mixed_ref[0, cols, width : 2 * width]
        value = mixed_ref[0, cols, 2 * width : 3 * width]
        add_query = add_key = add_value = None
        for head in range(heads):
            query = query_heads[head, rows, :]
            grad = grad_heads[head, rows, :]
            probs = jnp.exp(dot_nt(key, query) - log_ref[0, head : head + 1, rows])
            if on_diagonal:
                key_pos = lax.broadcasted_iota(jnp.int32, (block, block), 0)
                row_pos = lax.broadcasted_iota(jnp.int32, (block, block), 1)
                probs = jnp.where(row_pos >= key_pos, probs, 0.0)
            grad_probs = dot_nt(value, grad)
            grad_scores = (probs * (grad_probs - inner_rows[head : head + 1, rows])).astype(BF16)
            one_value = dot_nn(probs.astype(BF16), grad)
            one_key = dot_nn(grad_scores, query)
            one_query = dot_tn(grad_scores, key_heads[head, cols, :])
            add_value = one_value if head == 0 else add_value + one_value
            add_key = one_key if head == 0 else add_key + one_key
            add_query = one_query if head == 0 else add_query + one_query
        grad_value[cols, :] += add_value
        grad_key[cols, :] += add_key
        grad_query[rows, :] += add_query

    def row_step(row_block, carry):
        def col_step(col_block, inner_carry):
            tile(row_block, col_block, False)
            return inner_carry

        lax.fori_loop(0, row_block, col_step, 0)
        tile(row_block, row_block, True)
        return carry

    lax.fori_loop(0, blocks, row_step, 0)

    def finish(index, carry):
        rows = pl.ds(pl.multiple_of(index * block, block), block)
        pieces = (grad_query[rows, :] * SCALE, grad_key[rows, :], grad_value[rows, :])
        for place, piece in enumerate(pieces):
            piece = piece.astype(BF16)
            columns_here = slice(place * width, (place + 1) * width)
            result_ref[0, rows, columns_here] = piece
            sum_ref[0, 0:1, columns_here] += jnp.sum(piece.astype(F32), axis=0, keepdims=True)
        return carry

    sum_ref[...] = jnp.zeros_like(sum_ref)
    lax.fori_loop(0, blocks, finish, 0)


def attend_back(mixed, attended, grad_attended, logs, width):
    seqs, length, _ = mixed.shape
    heads = width // HEAD_DIM
    block = min(512, length)
    return pl.pallas_call(
        functools.partial(attend_back_kernel, block=block, width=width),
        grid=(seqs,),
        in_specs=[
            pl.BlockSpec((1, length, 3 * width), lambda s: (s, 0, 0)),
            pl.BlockSpec((1, length, width), lambda s: (s, 0, 0)),
            pl.BlockSpec((1, length, width), lambda s: (s, 0, 0)),
            pl.BlockSpec((1, LOG_ROWS, length), lambda s: (s, 0, 0)),
        ],
        out_specs=[
            pl.BlockSpec((1, length, 3 * width), lambda s: (s, 0, 0)),
            pl.BlockSpec((1, 8, 3 * width), lambda s: (s, 0, 0)),
        ],
        out_shape=[
            jax.ShapeDtypeStruct((seqs, length, 3 * width), BF16),
            jax.ShapeDtypeStruct((seqs, 8, 3 * width), F32),
        ],
        scratch_shapes=[
            pltpu.VMEM((heads, length, width), BF16),
            pltpu.VMEM((heads, length, width), BF16),
            pltpu.VMEM((heads, length, width), BF16),
            pltpu.VMEM((length, width), F32),
            pltpu.VMEM((length, width), F32),
            pltpu.VMEM((length, width), F32),
            pltpu.VMEM((LOG_ROWS, length), F32),
        ],
        compiler_params=pltpu.CompilerParams(vmem_limit_bytes=VMEM_BYTES),
        cost_estimate=pl.CostEstimate(
            flops=56 * seqs * length * length * width,
            bytes_accessed=16 * seqs * length * width,
            transcendentals=seqs * length * length * width // HEAD_DIM // 2,
        ),
    )(mixed, attended, grad_attended, logs)


def feed_kernel(*refs, parts, steps):
    normed_refs, rest = (refs[:parts], refs[parts:])
    cot_ref, fc_ref, proj_ref, bias_ref, active_ref, grad_ref = rest[:6]
    back_refs, ahead_refs = (rest[6 : 6 + parts], rest[6 + parts : 6 + 2 * parts])
    sum_ref = rest[6 + 2 * parts]
    index = pl.program_id(0)
    normed = normed_refs[0][...]
    for place in range(1, parts):
        normed = jnp.where(index >= place * steps, normed_refs[place][...], normed)
    hidden = dot_nn(normed, fc_ref[...]) + bias_ref[...]
    grad_active = dot_nt(cot_ref[...], proj_ref[...])
    square = hidden * hidden
    curve = jnp.tanh(ROOT_COEF * hidden * (1.0 + 0.044715 * square))
    half = 0.5 + 0.5 * curve
    active = (hidden * half).astype(BF16)
    slope = half + hidden * (0.5 - 0.5 * curve * curve) * (
        ROOT_COEF + (3.0 * 0.044715 * ROOT_COEF) * square
    )
    grad = (grad_active * slope).astype(BF16)
    active_ref[...] = active
    grad_ref[...] = grad
    back = dot_nt(grad, fc_ref[...]).astype(BF16)
    ahead = dot_nn(active, proj_ref[...]).astype(BF16)
    for place in range(parts):

        @pl.when(jnp.logical_and(index >= place * steps, index < (place + 1) * steps))
        def _(place=place):
            back_refs[place][...] = back
            ahead_refs[place][...] = ahead

    sums = jnp.sum(grad.astype(F32), axis=0, keepdims=True)

    @pl.when(index == 0)
    def _():
        sum_ref[...] = jnp.zeros_like(sum_ref)

    sum_ref[...] += sums


def feed(blocks, cotangent, weights, bias, width):
    rows, model = blocks[0].shape
    parts = len(blocks)
    block = min(256, rows)
    steps = rows // block

    def part_spec(place):
        return pl.BlockSpec((block, model), lambda i: (jnp.clip(i - place * steps, 0, steps - 1), 0))

    part_specs = [part_spec(place) for place in range(parts)]
    part_shapes = [jax.ShapeDtypeStruct((rows, model), BF16)] * parts
    wide_spec = pl.BlockSpec((block, width), lambda i: (i, 0))
    wide_shape = jax.ShapeDtypeStruct((parts * rows, width), BF16)
    if isinstance(weights, tuple):
        share_fc, share_proj = weights
        proj_place = 0
    else:
        share_fc = share_proj = weights
        proj_place = 1
    results = pl.pallas_call(
        functools.partial(feed_kernel, parts=parts, steps=steps),
        grid=(parts * steps,),
        in_specs=part_specs
        + [
            pl.BlockSpec((block, model), lambda i: (i, 0)),
            pl.BlockSpec((model, width), lambda i: (0, 0)),
            pl.BlockSpec((width, model), lambda i: (0, proj_place)),
            pl.BlockSpec((1, width), lambda i: (0, 0)),
        ],
        out_specs=[wide_spec, wide_spec]
        + part_specs
        + part_specs
        + [pl.BlockSpec((1, width), lambda i: (0, 0))],
        out_shape=[wide_shape, wide_shape]
        + part_shapes
        + part_shapes
        + [jax.ShapeDtypeStruct((1, width), F32)],
        compiler_params=pltpu.CompilerParams(vmem_limit_bytes=VMEM_BYTES),
        cost_estimate=pl.CostEstimate(
            flops=14 * parts * rows * model * width,
            bytes_accessed=parts * rows * (8 * model + 4 * width) + 4 * model * width,
            transcendentals=parts * rows * width,
        ),
    )(*blocks, cotangent, share_fc, share_proj, bias)
    back, ahead = (results[2 : 2 + parts], results[2 + parts : 2 + 2 * parts])
    return results[0], results[1], back, ahead, results[2 + 2 * parts]


def ring_order(shards):
    fast = 1
    while fast * fast * 4 <= shards:
        fast *= 2
    slow = shards // fast
    if fast == 1:
        return list(range(shards))
    path = [row * fast for row in range(slow)]
    for row in reversed(range(slow)):
        line = range(1, fast) if (slow - 1 - row) % 2 == 0 else reversed(range(1, fast))
        path += [row * fast + place for place in line]
    return path


def ring_move(array, towards):
    order = ring_order(lax.axis_size("dp"))
    shards = len(order)
    pairs = [(order[i], order[(i + towards) % shards]) for i in range(shards)]
    return lax.ppermute(array, "dp", pairs)


def ring_lookup(distance):
    order = ring_order(lax.axis_size("dp"))
    shards = len(order)
    own = lax.axis_index("dp")
    found = jnp.int32(order[distance % shards])
    for place in range(1, shards):
        found = jnp.where(own == order[place], order[(place + distance) % shards], found)
    return found


def ring_gather(share, ties, made):
    shards = lax.axis_size("dp")
    full = jnp.zeros((shards,) + share.shape, share.dtype)
    full = lax.dynamic_update_index_in_dim(full, share, lax.axis_index("dp"), 0)
    upward = downward = share
    for step in range(1, shards // 2 + 1):
        upward = ring_move(upward, 1)
        if 2 * step < shards:
            downward = ring_move(downward, -1)
        full = lax.dynamic_update_index_in_dim(full, upward, ring_lookup(-step), 0)
        if 2 * step < shards:
            full = lax.dynamic_update_index_in_dim(full, downward, ring_lookup(step), 0)
        for name, make in ties.get(step, ()):
            upward, made[name] = lax.optimization_barrier((upward, make()))
    return full


def ring_scatter(parts, ties, made):
    shards = parts.shape[0]
    half = shards // 2

    def own(distance):
        return lax.dynamic_index_in_dim(parts, ring_lookup(distance), 0, keepdims=False)

    downward = upward = None
    for distance in range(half, 0, -1):
        held = own(-distance)
        if downward is not None:
            held = (held.astype(F32) + downward.astype(F32)).astype(BF16)
        for name, make in ties.get(distance, ()):
            held, made[name] = lax.optimization_barrier((held, make()))
        downward = ring_move(held, -1)
        if distance < half or 2 * half < shards:
            held = own(distance)
            if upward is not None:
                held = (held.astype(F32) + upward.astype(F32)).astype(BF16)
            upward = ring_move(held, 1)
    total = own(0).astype(F32) + downward.astype(F32)
    return total if upward is None else total + upward.astype(F32)


def swap(array, offset):
    ranks = lax.axis_size("seq")
    return lax.ppermute(array, "seq", [(rank, rank ^ offset) for rank in range(ranks)])


def bits_up():
    ranks, bits, bit = (lax.axis_size("seq"), [], 1)
    while bit < ranks:
        bits.append(bit)
        bit *= 2
    return bits


def gather_offsets(array, bits=None):
    found = {0: array}
    for bit in reversed(bits_up() if bits is None else bits):
        for offset in sorted(found):
            found[offset | bit] = swap(found[offset], bit)
    return [found[offset] for offset in range(len(found))]


def reduce_offsets(blocks, bits=None):
    left = dict(enumerate(blocks))
    for bit in bits_up() if bits is None else bits:
        for offset in sorted(left, reverse=True):
            if offset & bit:
                arrived = swap(left.pop(offset).astype(BF16), bit)
                left[offset ^ bit] = left[offset ^ bit].astype(F32) + arrived.astype(F32)
    return left[0]


def placed(blocks, axis):
    rank = lax.axis_index("seq")
    size = blocks[0].shape[axis]
    shape = list(blocks[0].shape)
    shape[axis] = size * len(blocks)
    full = jnp.zeros(shape, blocks[0].dtype)
    for offset, block in enumerate(blocks):
        full = lax.dynamic_update_slice_in_dim(full, block, (rank ^ offset) * size, axis)
    return full


def picked(array, axis):
    rank, ranks = (lax.axis_index("seq"), lax.axis_size("seq"))
    size = array.shape[axis] // ranks
    return [
        lax.dynamic_slice_in_dim(array, (rank ^ offset) * size, size, axis)
        for offset in range(ranks)
    ]


def columns_kernel(rank_ref, *refs, pieces, ranks):
    blocks, fulls = (refs[:ranks], refs[ranks:])
    for offset, block_ref in enumerate(blocks):
        owner = lax.bitwise_xor(rank_ref[0, 0], offset)
        for (first, groups, size), full_ref in zip(pieces, fulls):
            for group in range(groups):
                start = pl.multiple_of((owner + group * ranks) * size, size)
                place = first + group * size
                piece = block_ref[0 : full_ref.shape[0], place : place + size]
                full_ref[:, pl.ds(start, size)] = piece.astype(full_ref.dtype)


def columns(blocks, pieces, dtype, rows=None):
    rows = blocks[0].shape[0] if rows is None else rows
    ranks = len(blocks)
    rank = lax.axis_index("seq")
    if any(size % 128 for _, _, size in pieces):
        results = []
        for first, groups, size in pieces:
            shaped = [
                block[:rows, first : first + groups * size].reshape(rows, groups, 1, size)
                for block in blocks
            ]
            results.append(placed(shaped, 2).reshape(rows, ranks * groups * size).astype(dtype))
        return results
    wide = sum(groups * size for _, groups, size in pieces) * ranks
    return pl.pallas_call(
        functools.partial(columns_kernel, pieces=pieces, ranks=ranks),
        in_specs=[pl.BlockSpec(memory_space=pltpu.SMEM)]
        + [pl.BlockSpec(memory_space=pltpu.VMEM)] * ranks,
        out_specs=[pl.BlockSpec(memory_space=pltpu.VMEM)] * len(pieces),
        out_shape=[
            jax.ShapeDtypeStruct((rows, ranks * groups * size), dtype)
            for _, groups, size in pieces
        ],
        compiler_params=pltpu.CompilerParams(vmem_limit_bytes=VMEM_BYTES),
        cost_estimate=pl.CostEstimate(
            flops=rows * wide, bytes_accessed=6 * rows * wide, transcendentals=0
        ),
    )(rank.astype(jnp.int32).reshape(1, 1), *blocks)


def row_stats(values):
    average = jnp.mean(values, axis=-1, keepdims=True)
    centered = values - average
    variance = jnp.mean(centered * centered, axis=-1, keepdims=True)
    inverse = lax.rsqrt(variance + EPSILON)
    return centered * inverse, inverse


def norm_back(incoming, gain, unit, inverse):
    scaled = incoming * gain
    first = jnp.mean(scaled, axis=-1, keepdims=True)
    second = jnp.mean(scaled * unit, axis=-1, keepdims=True)
    return inverse * (scaled - first - unit * second)


def vector_rows(vectors, columns_count):
    size = max(item.shape[1] for item in vectors)
    stacked = jnp.stack(
        [jnp.pad(item, ((0, 0), (0, size - item.shape[1]))) for item in vectors], axis=1
    )
    return jnp.pad(
        stacked, ((0, 0), (0, -stacked.shape[1] % 16), (0, columns_count - size))
    )


def per_device(
    tokens,
    cotangent,
    w_qkv,
    w_attn,
    w_fc,
    w_proj,
    bias_query,
    bias_value,
    bias_attn,
    gain_one,
    shift_one,
    gain_two,
    shift_two,
    bias_fc,
    bias_proj,
):
    ranks = lax.axis_size("seq")
    shards = lax.axis_size("dp")
    rank = lax.axis_index("seq")
    seqs, rows, model = tokens.shape
    length = rows * ranks
    width = model // ranks
    part = w_qkv.shape[0]
    hidden_part = w_proj.shape[0]
    units = hidden_part // ranks
    hidden_width = w_fc.shape[1] // ranks
    tokens_own = tokens.reshape(seqs * rows, model)
    cot_own = cotangent.reshape(seqs * rows, model)
    gather_columns = 4 * width
    *low_bits, top_bit = bits_up()

    def share_of(array, groups):
        size = array.shape[1] // (groups * ranks)
        return [
            lax.dynamic_slice_in_dim(array, (group * ranks + rank) * size, size, 1)
            for group in range(groups)
        ]

    vectors = [
        item.reshape(1, part)
        for item in (
            bias_query,
            bias_value,
            bias_attn,
            gain_one,
            shift_one,
            gain_two,
            shift_two,
            bias_proj,
        )
    ] + [item.reshape(1, units) for item in jnp.split(bias_fc, ranks)]
    packed = jnp.concatenate(
        [
            jnp.concatenate(share_of(w_qkv, 3) + share_of(w_attn, 1), axis=1),
            vector_rows(vectors, gather_columns)[0],
        ],
        axis=0,
    )

    token_blocks = gather_offsets(tokens)
    steps = shards // 2
    middle_step = max(2, steps // 2)
    made = {}

    def feed_share():
        wide, tall = made["feed"]
        tall = lax.dynamic_slice_in_dim(tall, rank * units, units, 0)
        tall = tall.reshape(part, units * model // part)
        return jnp.concatenate(share_of(wide, shards) + [tall], axis=1)

    full = ring_gather(
        packed,
        {
            1: [("feed", lambda: (w_fc, w_proj))],
            middle_step: [("tokens", lambda: token_blocks)],
            steps - 1: [("share", feed_share)],
        },
        made,
    )
    token_blocks = made["tokens"]
    second_gather = lax.all_gather(made["share"], "dp", axis=0)
    if units == part and hidden_width == model:
        feed_weights = second_gather.reshape(model, 2 * model)
    else:
        feed_weights = (
            second_gather[:, :, :hidden_width].reshape(model, hidden_width),
            second_gather[:, :, hidden_width:].reshape(hidden_width, model),
        )
    full_qkv = full[:, :part, : 3 * width].reshape(model, 3 * width)
    attn_columns = full[:, :part, 3 * width :].reshape(model, width)
    vector_block = full[:, part:].astype(F32)

    def vector(index):
        return vector_block[:, index, :part].reshape(model)

    query_bias = lax.dynamic_slice_in_dim(vector(0), rank * width, width)
    value_bias = lax.dynamic_slice_in_dim(vector(1), rank * width, width)
    attn_bias = vector(2)
    gain_first, shift_first, gain_second, shift_second, proj_bias = (
        vector(3),
        vector(4),
        vector(5),
        vector(6),
        vector(7),
    )
    fc_bias = lax.dynamic_index_in_dim(vector_block, 8 + rank, 1, keepdims=False)
    fc_bias = fc_bias[:, :units].reshape(hidden_width)
    half = ranks // 2
    joint_bias = jnp.concatenate([query_bias, jnp.zeros_like(query_bias), value_bias])
    normed, mixed = project(token_blocks, full_qkv, gain_first, shift_first, joint_bias)
    normed = normed.reshape(seqs * length, model)
    mixed = mixed.reshape(seqs, length, 3 * width)
    mixed, cot_sent, attn_columns, attn_far = lax.optimization_barrier(
        (mixed, cot_own, attn_columns, swap(attn_columns, top_bit))
    )
    cot_far = swap(cot_sent, top_bit)
    attended, logs = attend(mixed, width)
    attended, cot_far, cot_near = lax.optimization_barrier((attended, cot_far, cot_own))
    near_cot = jnp.concatenate(gather_offsets(cot_near, low_bits), axis=0)
    far_cot = jnp.concatenate(gather_offsets(cot_far, low_bits), axis=0)

    sent = picked(attended, 1)
    arrived = [sent[0]] + [swap(sent[offset], offset) for offset in range(1, ranks)]
    attn_blocks = gather_offsets(attn_columns, low_bits) + gather_offsets(attn_far, low_bits)
    (full_attn,) = columns(attn_blocks, ((0, 1, width),), BF16)
    arrived, full_attn, near_cot, far_cot = lax.optimization_barrier(
        (arrived, full_attn, near_cot, far_cot)
    )
    (joined,) = columns(
        [item.reshape(seqs * rows, width) for item in arrived], ((0, 1, width),), BF16
    )

    inputs = tokens_own.astype(F32)
    middle = inputs + (dot_nn(joined, full_attn) + attn_bias)
    unit_two, inverse_two = row_stats(middle)
    normed_two = (unit_two * gain_second + shift_second).astype(BF16)
    near_blocks = gather_offsets(normed_two, low_bits)
    far_own = swap(normed_two, top_bit)
    feed_bias = fc_bias.reshape(1, hidden_width)
    near_active, near_grad, near_back, near_ahead, near_sum = feed(
        near_blocks, near_cot, feed_weights, feed_bias, hidden_width
    )
    far_own, near_active = lax.optimization_barrier((far_own, near_active))
    far_blocks = gather_offsets(far_own, low_bits)
    far_active, far_grad, far_back, far_ahead, far_sum = feed(
        far_blocks, far_cot, feed_weights, feed_bias, hidden_width
    )
    near_part = reduce_offsets(near_back, low_bits)
    far_part = reduce_offsets(far_back, low_bits).astype(BF16)
    far_part, far_active, far_grad = lax.optimization_barrier((far_part, far_active, far_grad))
    grad_normed_two = near_part.astype(F32) + swap(far_part, top_bit).astype(F32)
    near_two = jnp.concatenate(near_blocks, axis=0)
    far_two = jnp.concatenate(far_blocks, axis=0)

    upstream = cot_own.astype(F32)
    grad_w_proj = dot_tn(near_active, near_cot) + dot_tn(far_active, far_cot)
    grad_w_proj = grad_w_proj.astype(BF16).reshape(shards, part, units * model // part)
    grad_w_fc = dot_tn(near_two, near_grad) + dot_tn(far_two, far_grad)
    grad_w_fc = grad_w_fc.astype(BF16).reshape(shards, part, hidden_width)
    grad_bias_fc = (near_sum + far_sum).reshape(hidden_width)
    grad_bias_proj = jnp.sum(upstream, axis=0)
    first_parts = jnp.concatenate([grad_w_fc, grad_w_proj], axis=2)
    first_scatter = lax.psum_scatter(first_parts, "dp", scatter_dimension=0)
    grad_normed_two, _ = lax.optimization_barrier((grad_normed_two, first_parts))
    grad_gain_two = jnp.sum(grad_normed_two * unit_two, axis=0)
    grad_shift_two = jnp.sum(grad_normed_two, axis=0)
    grad_middle = upstream + norm_back(grad_normed_two, gain_second, unit_two, inverse_two)
    grad_branch = grad_middle.astype(BF16)
    grad_joined = dot_nt(grad_branch, full_attn).astype(BF16)
    grad_sent = picked(grad_joined.reshape(seqs, rows, model), 2)
    grad_arrived = [grad_sent[0]] + [
        swap(grad_sent[offset], offset) for offset in range(1, ranks)
    ]
    grad_attended = placed(grad_arrived, 1)

    ahead, _ = lax.optimization_barrier(((near_ahead, far_ahead), grad_branch))
    near_ahead, far_ahead = ahead
    ahead_far = reduce_offsets(far_ahead, low_bits).astype(BF16)
    grad_attn_part = picked(dot_tn(joined, grad_branch).astype(BF16), 1)
    attn_near = reduce_offsets(grad_attn_part[:half], low_bits)
    attn_far = reduce_offsets(grad_attn_part[half:], low_bits).astype(BF16)
    grad_attended, ahead_far, attn_far, attn_near = lax.optimization_barrier(
        (grad_attended, ahead_far, attn_far, attn_near)
    )
    ahead_far = swap(ahead_far, top_bit)
    attn_far = swap(attn_far, top_bit)
    ahead_part = reduce_offsets(near_ahead, low_bits)
    grad_w_attn = (attn_near.astype(F32) + attn_far.astype(F32)).astype(BF16)
    grad_bias_attn = jnp.sum(grad_branch, axis=0, dtype=F32)

    grad_mixed, column_sums = attend_back(mixed, attended, grad_attended, logs, width)
    grad_mixed = grad_mixed.reshape(seqs * length, 3 * width)
    grad_w_qkv = dot_tn(normed, grad_mixed)
    column_sums = jnp.sum(column_sums[:, 0], axis=0)
    qkv_values = full_qkv.astype(F32)
    grad_shift_one = jnp.sum(qkv_values * column_sums, axis=1)
    grad_gain_one = (
        jnp.sum(qkv_values * grad_w_qkv, axis=1) - shift_first * grad_shift_one
    ) / gain_first

    def spread(values):
        return lax.dynamic_update_slice_in_dim(
            jnp.zeros((model,), F32), values, rank * width, 0
        )

    grad_vectors = [
        item.reshape(shards, -1).astype(BF16)
        for item in (
            spread(column_sums[:width]),
            spread(column_sums[2 * width :]),
            grad_bias_attn,
            grad_gain_one,
            grad_shift_one,
            grad_gain_two,
            grad_shift_two,
            grad_bias_proj,
            grad_bias_fc,
        )
    ]
    last_parts = jnp.concatenate(
        [
            jnp.concatenate(
                [
                    grad_w_qkv.astype(BF16).reshape(shards, part, 3 * width),
                    grad_w_attn.reshape(shards, part, width),
                ],
                axis=2,
            ),
            vector_rows(grad_vectors, gather_columns),
        ],
        axis=1,
    )
    made = {}

    def far_sum():
        back = dot_nt(made["mixed"], full_qkv).astype(BF16).reshape(seqs, length, model)
        blocks = [item.reshape(seqs * rows, model) for item in picked(back, 1)]
        far = reduce_offsets(blocks[half:], low_bits).astype(BF16)
        near, far = lax.optimization_barrier((blocks[:half], far))
        made["near"] = reduce_offsets(near, low_bits)
        return far

    last_scatter = ring_scatter(
        last_parts,
        {
            steps: [("mixed", lambda: grad_mixed)],
            max(steps - 1, 1): [("far", far_sum)],
            max(steps - 2, 1): [("scatter", lambda: first_scatter)],
        },
        made,
    )
    far_arrived = swap(made["far"], top_bit)
    fed_far = swap(made["scatter"], top_bit)
    last_scatter = last_scatter.astype(BF16)
    far_arrived, fed_far, _ = lax.optimization_barrier((far_arrived, fed_far, last_scatter))
    grad_normed = made["near"].astype(F32) + far_arrived.astype(F32)
    fed = gather_offsets(made["scatter"], low_bits) + gather_offsets(fed_far, low_bits)
    rest = gather_offsets(last_scatter)

    _, ahead_far = lax.optimization_barrier((grad_mixed, ahead_far))
    output = (middle + ahead_part.astype(F32) + ahead_far.astype(F32) + proj_bias).astype(BF16)
    unit_one, inverse_one = row_stats(inputs)
    grad_tokens = grad_middle + norm_back(grad_normed, gain_first, unit_one, inverse_one)

    (out_fc,) = columns(fed, ((0, shards, units),), F32)
    proj_blocks = [item[:, hidden_width:].reshape(units, model) for item in fed]
    out_proj = placed(proj_blocks, 0).astype(F32)
    out_qkv, out_attn = columns(rest, ((0, 3, width), (3 * width, 1, width)), F32, part)
    tails = [item[part:].astype(F32) for item in rest]
    summed = sum(tails)[:, :part]
    out_bias_fc = placed([item[8, :units] for item in tails], 0)

    def out_vector(index):
        return summed[index]

    return (
        output.reshape(seqs, rows, model),
        grad_tokens.reshape(seqs, rows, model),
        out_qkv,
        out_attn,
        out_fc,
        out_proj,
        out_vector(0),
        out_vector(1),
        out_vector(2),
        out_vector(3),
        out_vector(4),
        out_vector(5),
        out_vector(6),
        out_bias_fc,
        out_vector(7),
    )


def solution(mesh):
    token_spec = P("dp", "seq", None)
    in_specs = (token_spec,) * 2 + (P("dp", None),) * 4 + (P("dp"),) * 9
    out_specs = (token_spec,) * 2 + (P("dp", None),) * 4 + (P("dp"),) * 9
    return jax.shard_map(
        per_device, mesh=mesh, in_specs=in_specs, out_specs=out_specs, check_vma=False
    )
```

```python
import functools

import jax
import jax.numpy as jnp
from jax import lax
from jax.experimental import pallas as pl
from jax.experimental.pallas import tpu as pltpu
from jax.sharding import PartitionSpec as P

HEAD_DIM = 64
EPSILON = 1e-05
ROOT_COEF = 0.7978845608028654
SCALE = HEAD_DIM ** (-0.5)
BF16 = jnp.bfloat16
F32 = jnp.float32
LOG_ROWS = 8
VMEM_BYTES = 56 * 1024 * 1024


def gelu_tanh(values):
    return (
        0.5 * values * (1.0 + jnp.tanh(ROOT_COEF * (values + 0.044715 * values * values * values)))
    )


def dot_nn(left_side, right_side):
    return lax.dot_general(
        left_side, right_side, (((1,), (0,)), ((), ())), preferred_element_type=F32
    )


def dot_nt(left_side, right_side):
    return lax.dot_general(
        left_side, right_side, (((1,), (1,)), ((), ())), preferred_element_type=F32
    )


def dot_tn(left_side, right_side):
    return lax.dot_general(
        left_side, right_side, (((0,), (0,)), ((), ())), preferred_element_type=F32
    )


def project_kernel(rank_ref, *refs, parts):
    del rank_ref
    block_refs = refs[:parts]
    weight_ref, gain_ref, shift_ref, bias_ref, normed_ref, mixed_ref = refs[parts:]
    place = pl.program_id(0)
    values = block_refs[0][0]
    for part in range(1, parts):
        values = jnp.where(place == part, block_refs[part][0], values)
    values = values.astype(F32)
    centered = values - jnp.mean(values, axis=-1, keepdims=True)
    inverse = lax.rsqrt(jnp.mean(centered * centered, axis=-1, keepdims=True) + EPSILON)
    normed = (centered * inverse * gain_ref[...] + shift_ref[...]).astype(BF16)
    normed_ref[0, 0] = normed
    mixed_ref[0, 0] = (dot_nn(normed, weight_ref[...]) + bias_ref[...]).astype(BF16)


def project(blocks, weight, gain, shift, bias):
    seqs, rows, model = blocks[0].shape
    parts, wide = (len(blocks), weight.shape[1])
    block = min(256, rows)
    steps = rows // block

    def block_spec(part):
        def index_map(p, s, b, rank_ref):
            seq = jnp.where(p < part, 0, jnp.where(p > part, seqs - 1, s))
            row = jnp.where(p < part, 0, jnp.where(p > part, steps - 1, b))
            return (seq, row, 0)

        return pl.BlockSpec((1, block, model), index_map)

    def whole_spec(*shape):
        return pl.BlockSpec(shape, lambda p, s, b, rank_ref: (0, 0))

    def out_spec(columns_count):
        return pl.BlockSpec(
            (1, 1, block, columns_count),
            lambda p, s, b, rank_ref: (s, lax.bitwise_xor(rank_ref[0], p), b, 0),
        )

    return pl.pallas_call(
        functools.partial(project_kernel, parts=parts),
        grid_spec=pltpu.PrefetchScalarGridSpec(
            num_scalar_prefetch=1,
            grid=(parts, seqs, steps),
            in_specs=[block_spec(part) for part in range(parts)]
            + [
                whole_spec(model, wide),
                whole_spec(1, model),
                whole_spec(1, model),
                whole_spec(1, wide),
            ],
            out_specs=[out_spec(model), out_spec(wide)],
        ),
        out_shape=[
            jax.ShapeDtypeStruct((seqs, parts, rows, model), BF16),
            jax.ShapeDtypeStruct((seqs, parts, rows, wide), BF16),
        ],
        compiler_params=pltpu.CompilerParams(vmem_limit_bytes=VMEM_BYTES),
        cost_estimate=pl.CostEstimate(
            flops=4 * parts * seqs * rows * model * wide,
            bytes_accessed=parts * seqs * rows * (4 * model + 2 * wide) + 2 * model * wide,
            transcendentals=parts * seqs * rows,
        ),
    )(
        lax.axis_index("seq").astype(jnp.int32).reshape(1),
        *blocks,
        weight,
        gain.reshape(1, model),
        shift.reshape(1, model),
        bias.reshape(1, wide),
    )


def head_lanes(array, head):
    lanes = lax.broadcasted_iota(jnp.int32, array.shape, 1)
    owner = lax.shift_right_logical(lanes, 6)
    return jnp.where(owner == head, array.astype(F32), 0.0)


def attend_kernel(mixed_ref, out_ref, log_ref, *, block, width):
    length = mixed_ref.shape[1]
    heads = width // HEAD_DIM
    step = 4 if heads % 4 == 0 else 1
    for index in range(length // block):
        first, stop = index * block, (index + 1) * block
        query = mixed_ref[0, first:stop, 0:width]
        row_pos = lax.broadcasted_iota(jnp.int32, (block, block), 0)
        col_pos = lax.broadcasted_iota(jnp.int32, (block, block), 1)
        allowed = row_pos >= col_pos
        log_lanes = lax.broadcasted_iota(jnp.int32, (block, 128), 1)

        def one_head(head, carry):
            total, logs = carry
            masked = (head_lanes(query, head) * SCALE).astype(BF16)
            diagonal = dot_nt(masked, mixed_ref[0, first:stop, width : 2 * width])
            diagonal = jnp.where(allowed, diagonal, -1e30)
            largest = jnp.max(diagonal, axis=1, keepdims=True)
            if first:
                scores = dot_nt(masked, mixed_ref[0, 0:first, width : 2 * width])
                largest = jnp.maximum(largest, jnp.max(scores, axis=1, keepdims=True))
            weights = jnp.exp(diagonal - largest)
            row_total = jnp.sum(weights, axis=1, keepdims=True)
            mixed = dot_nn(
                weights.astype(BF16), mixed_ref[0, first:stop, 2 * width : 3 * width]
            )
            if first:
                weights = jnp.exp(scores - largest)
                row_total = row_total + jnp.sum(weights, axis=1, keepdims=True)
                mixed = mixed + dot_nn(
                    weights.astype(BF16), mixed_ref[0, 0:first, 2 * width : 3 * width]
                )
            total = total + head_lanes(mixed * (1.0 / row_total), head)
            logs = jnp.where(log_lanes == head, largest + jnp.log(row_total), logs)
            return (total, logs)

        def some_heads(group, carry):
            for inner in range(step):
                carry = one_head(group * step + inner, carry)
            return carry

        total, logs = lax.fori_loop(
            0,
            heads // step,
            some_heads,
            (jnp.zeros((block, width), F32), jnp.zeros((block, 128), F32)),
        )
        out_ref[0, first:stop, :] = total.astype(BF16)
        log_ref[0, :, first:stop] = jnp.transpose(logs)[0:LOG_ROWS]


def attend(mixed, width):
    seqs, length, _ = mixed.shape
    block = min(256, length)
    return pl.pallas_call(
        functools.partial(attend_kernel, block=block, width=width),
        grid=(seqs,),
        in_specs=[pl.BlockSpec((1, length, 3 * width), lambda s: (s, 0, 0))],
        out_specs=[
            pl.BlockSpec((1, length, width), lambda s: (s, 0, 0)),
            pl.BlockSpec((1, LOG_ROWS, length), lambda s: (s, 0, 0)),
        ],
        out_shape=[
            jax.ShapeDtypeStruct((seqs, length, width), BF16),
            jax.ShapeDtypeStruct((seqs, LOG_ROWS, length), F32),
        ],
        compiler_params=pltpu.CompilerParams(vmem_limit_bytes=VMEM_BYTES),
        cost_estimate=pl.CostEstimate(
            flops=28 * seqs * length * length * width,
            bytes_accessed=8 * seqs * length * width,
            transcendentals=seqs * length * length * width // HEAD_DIM // 2,
        ),
    )(mixed)


def attend_back_kernel(
    mixed_ref,
    out_ref,
    grad_ref,
    log_ref,
    result_ref,
    sum_ref,
    query_heads,
    key_heads,
    grad_heads,
    grad_query,
    grad_key,
    grad_value,
    inner_rows,
    *,
    block,
    width,
):
    length = mixed_ref.shape[1]
    heads = width // HEAD_DIM
    blocks = length // block
    owner = lax.shift_right_logical(lax.broadcasted_iota(jnp.int32, (LOG_ROWS, width), 1), 6)
    picks = (owner == lax.broadcasted_iota(jnp.int32, (LOG_ROWS, width), 0)).astype(F32)

    def prepare(index, carry):
        rows = pl.ds(pl.multiple_of(index * block, block), block)
        query = mixed_ref[0, rows, 0:width]
        key = mixed_ref[0, rows, width : 2 * width]
        grad = grad_ref[0, rows, :]
        for head in range(heads):
            query_heads[head, rows, :] = (head_lanes(query, head) * SCALE).astype(BF16)
            key_heads[head, rows, :] = head_lanes(key, head).astype(BF16)
            grad_heads[head, rows, :] = head_lanes(grad, head).astype(BF16)
        product = grad.astype(F32) * out_ref[0, rows, :].astype(F32)
        inner_rows[:, rows] = lax.dot_general(
            picks,
            product,
            (((1,), (1,)), ((), ())),
            precision=lax.Precision.HIGHEST,
            preferred_element_type=F32,
        )
        zeros = jnp.zeros((block, width), F32)
        grad_query[rows, :] = zeros
        grad_key[rows, :] = zeros
        grad_value[rows, :] = zeros
        return carry

    lax.fori_loop(0, blocks, prepare, 0)

    def tile(row_block, col_block, on_diagonal):
        rows = pl.ds(pl.multiple_of(row_block * block, block), block)
        cols = pl.ds(pl.multiple_of(col_block * block, block), block)
        key = mixed_ref[0, cols, width : 2 * width]
        value = mixed_ref[0, cols, 2 * width : 3 * width]
        add_query = add_key = add_value = None
        for head in range(heads):
            query = query_heads[head, rows, :]
            grad = grad_heads[head, rows, :]
            probs = jnp.exp(dot_nt(key, query) - log_ref[0, head : head + 1, rows])
            if on_diagonal:
                key_pos = lax.broadcasted_iota(jnp.int32, (block, block), 0)
                row_pos = lax.broadcasted_iota(jnp.int32, (block, block), 1)
                probs = jnp.where(row_pos >= key_pos, probs, 0.0)
            grad_probs = dot_nt(value, grad)
            grad_scores = (probs * (grad_probs - inner_rows[head : head + 1, rows])).astype(BF16)
            one_value = dot_nn(probs.astype(BF16), grad)
            one_key = dot_nn(grad_scores, query)
            one_query = dot_tn(grad_scores, key_heads[head, cols, :])
            add_value = one_value if head == 0 else add_value + one_value
            add_key = one_key if head == 0 else add_key + one_key
            add_query = one_query if head == 0 else add_query + one_query
        grad_value[cols, :] += add_value
        grad_key[cols, :] += add_key
        grad_query[rows, :] += add_query

    def row_step(row_block, carry):
        def col_step(col_block, inner_carry):
            tile(row_block, col_block, False)
            return inner_carry

        lax.fori_loop(0, row_block, col_step, 0)
        tile(row_block, row_block, True)
        return carry

    lax.fori_loop(0, blocks, row_step, 0)

    def finish(index, carry):
        rows = pl.ds(pl.multiple_of(index * block, block), block)
        pieces = (grad_query[rows, :] * SCALE, grad_key[rows, :], grad_value[rows, :])
        for place, piece in enumerate(pieces):
            piece = piece.astype(BF16)
            columns_here = slice(place * width, (place + 1) * width)
            result_ref[0, rows, columns_here] = piece
            sum_ref[0, 0:1, columns_here] += jnp.sum(piece.astype(F32), axis=0, keepdims=True)
        return carry

    sum_ref[...] = jnp.zeros_like(sum_ref)
    lax.fori_loop(0, blocks, finish, 0)


def attend_back(mixed, attended, grad_attended, logs, width):
    seqs, length, _ = mixed.shape
    heads = width // HEAD_DIM
    block = min(512, length)
    return pl.pallas_call(
        functools.partial(attend_back_kernel, block=block, width=width),
        grid=(seqs,),
        in_specs=[
            pl.BlockSpec((1, length, 3 * width), lambda s: (s, 0, 0)),
            pl.BlockSpec((1, length, width), lambda s: (s, 0, 0)),
            pl.BlockSpec((1, length, width), lambda s: (s, 0, 0)),
            pl.BlockSpec((1, LOG_ROWS, length), lambda s: (s, 0, 0)),
        ],
        out_specs=[
            pl.BlockSpec((1, length, 3 * width), lambda s: (s, 0, 0)),
            pl.BlockSpec((1, 8, 3 * width), lambda s: (s, 0, 0)),
        ],
        out_shape=[
            jax.ShapeDtypeStruct((seqs, length, 3 * width), BF16),
            jax.ShapeDtypeStruct((seqs, 8, 3 * width), F32),
        ],
        scratch_shapes=[
            pltpu.VMEM((heads, length, width), BF16),
            pltpu.VMEM((heads, length, width), BF16),
            pltpu.VMEM((heads, length, width), BF16),
            pltpu.VMEM((length, width), F32),
            pltpu.VMEM((length, width), F32),
            pltpu.VMEM((length, width), F32),
            pltpu.VMEM((LOG_ROWS, length), F32),
        ],
        compiler_params=pltpu.CompilerParams(vmem_limit_bytes=VMEM_BYTES),
        cost_estimate=pl.CostEstimate(
            flops=56 * seqs * length * length * width,
            bytes_accessed=16 * seqs * length * width,
            transcendentals=seqs * length * length * width // HEAD_DIM // 2,
        ),
    )(mixed, attended, grad_attended, logs)


def feed_kernel(*refs, parts, steps):
    normed_refs, rest = (refs[:parts], refs[parts:])
    cot_ref, fc_ref, proj_ref, bias_ref, active_ref, grad_ref = rest[:6]
    back_refs, ahead_refs = (rest[6 : 6 + parts], rest[6 + parts : 6 + 2 * parts])
    sum_ref = rest[6 + 2 * parts]
    index = pl.program_id(0)
    normed = normed_refs[0][...]
    for place in range(1, parts):
        normed = jnp.where(index >= place * steps, normed_refs[place][...], normed)
    hidden = dot_nn(normed, fc_ref[...]) + bias_ref[...]
    grad_active = dot_nt(cot_ref[...], proj_ref[...])
    square = hidden * hidden
    curve = jnp.tanh(ROOT_COEF * hidden * (1.0 + 0.044715 * square))
    half = 0.5 + 0.5 * curve
    active = (hidden * half).astype(BF16)
    slope = half + hidden * (0.5 - 0.5 * curve * curve) * (
        ROOT_COEF + (3.0 * 0.044715 * ROOT_COEF) * square
    )
    grad = (grad_active * slope).astype(BF16)
    active_ref[...] = active
    grad_ref[...] = grad
    back = dot_nt(grad, fc_ref[...]).astype(BF16)
    ahead = dot_nn(active, proj_ref[...]).astype(BF16)
    for place in range(parts):

        @pl.when(jnp.logical_and(index >= place * steps, index < (place + 1) * steps))
        def _(place=place):
            back_refs[place][...] = back
            ahead_refs[place][...] = ahead

    sums = jnp.sum(grad.astype(F32), axis=0, keepdims=True)

    @pl.when(index == 0)
    def _():
        sum_ref[...] = jnp.zeros_like(sum_ref)

    sum_ref[...] += sums


def feed(blocks, cotangent, weights, bias, width):
    rows, model = blocks[0].shape
    parts = len(blocks)
    block = min(256, rows)
    steps = rows // block

    def part_spec(place):
        return pl.BlockSpec((block, model), lambda i: (jnp.clip(i - place * steps, 0, steps - 1), 0))

    part_specs = [part_spec(place) for place in range(parts)]
    part_shapes = [jax.ShapeDtypeStruct((rows, model), BF16)] * parts
    wide_spec = pl.BlockSpec((block, width), lambda i: (i, 0))
    wide_shape = jax.ShapeDtypeStruct((parts * rows, width), BF16)
    if isinstance(weights, tuple):
        share_fc, share_proj = weights
        proj_place = 0
    else:
        share_fc = share_proj = weights
        proj_place = 1
    results = pl.pallas_call(
        functools.partial(feed_kernel, parts=parts, steps=steps),
        grid=(parts * steps,),
        in_specs=part_specs
        + [
            pl.BlockSpec((block, model), lambda i: (i, 0)),
            pl.BlockSpec((model, width), lambda i: (0, 0)),
            pl.BlockSpec((width, model), lambda i: (0, proj_place)),
            pl.BlockSpec((1, width), lambda i: (0, 0)),
        ],
        out_specs=[wide_spec, wide_spec]
        + part_specs
        + part_specs
        + [pl.BlockSpec((1, width), lambda i: (0, 0))],
        out_shape=[wide_shape, wide_shape]
        + part_shapes
        + part_shapes
        + [jax.ShapeDtypeStruct((1, width), F32)],
        compiler_params=pltpu.CompilerParams(vmem_limit_bytes=VMEM_BYTES),
        cost_estimate=pl.CostEstimate(
            flops=14 * parts * rows * model * width,
            bytes_accessed=parts * rows * (8 * model + 4 * width) + 4 * model * width,
            transcendentals=parts * rows * width,
        ),
    )(*blocks, cotangent, share_fc, share_proj, bias)
    back, ahead = (results[2 : 2 + parts], results[2 + parts : 2 + 2 * parts])
    return results[0], results[1], back, ahead, results[2 + 2 * parts]


def ring_order(shards):
    fast = 1
    while fast * fast * 4 <= shards:
        fast *= 2
    slow = shards // fast
    if fast == 1:
        return list(range(shards))
    path = [row * fast for row in range(slow)]
    for row in reversed(range(slow)):
        line = range(1, fast) if (slow - 1 - row) % 2 == 0 else reversed(range(1, fast))
        path += [row * fast + place for place in line]
    return path


def ring_move(array, towards):
    order = ring_order(lax.axis_size("dp"))
    shards = len(order)
    pairs = [(order[i], order[(i + towards) % shards]) for i in range(shards)]
    return lax.ppermute(array, "dp", pairs)


def ring_lookup(distance):
    order = ring_order(lax.axis_size("dp"))
    shards = len(order)
    own = lax.axis_index("dp")
    found = jnp.int32(order[distance % shards])
    for place in range(1, shards):
        found = jnp.where(own == order[place], order[(place + distance) % shards], found)
    return found


def ring_gather(share, ties, made):
    shards = lax.axis_size("dp")
    full = jnp.zeros((shards,) + share.shape, share.dtype)
    full = lax.dynamic_update_index_in_dim(full, share, lax.axis_index("dp"), 0)
    upward = downward = share
    for step in range(1, shards // 2 + 1):
        upward = ring_move(upward, 1)
        if 2 * step < shards:
            downward = ring_move(downward, -1)
        full = lax.dynamic_update_index_in_dim(full, upward, ring_lookup(-step), 0)
        if 2 * step < shards:
            full = lax.dynamic_update_index_in_dim(full, downward, ring_lookup(step), 0)
        for name, make in ties.get(step, ()):
            upward, made[name] = lax.optimization_barrier((upward, make()))
    return full


def ring_scatter(parts, ties, made):
    shards = parts.shape[0]
    half = shards // 2

    def own(distance):
        return lax.dynamic_index_in_dim(parts, ring_lookup(distance), 0, keepdims=False)

    downward = upward = None
    for distance in range(half, 0, -1):
        held = own(-distance)
        if downward is not None:
            held = (held.astype(F32) + downward.astype(F32)).astype(BF16)
        for name, make in ties.get(distance, ()):
            held, made[name] = lax.optimization_barrier((held, make()))
        downward = ring_move(held, -1)
        if distance < half or 2 * half < shards:
            held = own(distance)
            if upward is not None:
                held = (held.astype(F32) + upward.astype(F32)).astype(BF16)
            upward = ring_move(held, 1)
    total = own(0).astype(F32) + downward.astype(F32)
    return total if upward is None else total + upward.astype(F32)


def swap(array, offset):
    ranks = lax.axis_size("seq")
    return lax.ppermute(array, "seq", [(rank, rank ^ offset) for rank in range(ranks)])


def bits_up():
    ranks, bits, bit = (lax.axis_size("seq"), [], 1)
    while bit < ranks:
        bits.append(bit)
        bit *= 2
    return bits


def gather_offsets(array, bits=None):
    found = {0: array}
    for bit in reversed(bits_up() if bits is None else bits):
        for offset in sorted(found):
            found[offset | bit] = swap(found[offset], bit)
    return [found[offset] for offset in range(len(found))]


def reduce_offsets(blocks, bits=None):
    left = dict(enumerate(blocks))
    for bit in bits_up() if bits is None else bits:
        for offset in sorted(left, reverse=True):
            if offset & bit:
                arrived = swap(left.pop(offset).astype(BF16), bit)
                left[offset ^ bit] = left[offset ^ bit].astype(F32) + arrived.astype(F32)
    return left[0]


def placed(blocks, axis):
    rank = lax.axis_index("seq")
    size = blocks[0].shape[axis]
    shape = list(blocks[0].shape)
    shape[axis] = size * len(blocks)
    full = jnp.zeros(shape, blocks[0].dtype)
    for offset, block in enumerate(blocks):
        full = lax.dynamic_update_slice_in_dim(full, block, (rank ^ offset) * size, axis)
    return full


def picked(array, axis):
    rank, ranks = (lax.axis_index("seq"), lax.axis_size("seq"))
    size = array.shape[axis] // ranks
    return [
        lax.dynamic_slice_in_dim(array, (rank ^ offset) * size, size, axis)
        for offset in range(ranks)
    ]


def columns_kernel(rank_ref, *refs, pieces, ranks):
    blocks, fulls = (refs[:ranks], refs[ranks:])
    for offset, block_ref in enumerate(blocks):
        owner = lax.bitwise_xor(rank_ref[0, 0], offset)
        for (first, groups, size), full_ref in zip(pieces, fulls):
            for group in range(groups):
                start = pl.multiple_of((owner + group * ranks) * size, size)
                place = first + group * size
                piece = block_ref[0 : full_ref.shape[0], place : place + size]
                full_ref[:, pl.ds(start, size)] = piece.astype(full_ref.dtype)


def columns(blocks, pieces, dtype, rows=None):
    rows = blocks[0].shape[0] if rows is None else rows
    ranks = len(blocks)
    rank = lax.axis_index("seq")
    if any(size % 128 for _, _, size in pieces):
        results = []
        for first, groups, size in pieces:
            shaped = [
                block[:rows, first : first + groups * size].reshape(rows, groups, 1, size)
                for block in blocks
            ]
            results.append(placed(shaped, 2).reshape(rows, ranks * groups * size).astype(dtype))
        return results
    wide = sum(groups * size for _, groups, size in pieces) * ranks
    return pl.pallas_call(
        functools.partial(columns_kernel, pieces=pieces, ranks=ranks),
        in_specs=[pl.BlockSpec(memory_space=pltpu.SMEM)]
        + [pl.BlockSpec(memory_space=pltpu.VMEM)] * ranks,
        out_specs=[pl.BlockSpec(memory_space=pltpu.VMEM)] * len(pieces),
        out_shape=[
            jax.ShapeDtypeStruct((rows, ranks * groups * size), dtype)
            for _, groups, size in pieces
        ],
        compiler_params=pltpu.CompilerParams(vmem_limit_bytes=VMEM_BYTES),
        cost_estimate=pl.CostEstimate(
            flops=rows * wide, bytes_accessed=6 * rows * wide, transcendentals=0
        ),
    )(rank.astype(jnp.int32).reshape(1, 1), *blocks)


def row_stats(values):
    average = jnp.mean(values, axis=-1, keepdims=True)
    centered = values - average
    variance = jnp.mean(centered * centered, axis=-1, keepdims=True)
    inverse = lax.rsqrt(variance + EPSILON)
    return centered * inverse, inverse


def norm_back(incoming, gain, unit, inverse):
    scaled = incoming * gain
    first = jnp.mean(scaled, axis=-1, keepdims=True)
    second = jnp.mean(scaled * unit, axis=-1, keepdims=True)
    return inverse * (scaled - first - unit * second)


def vector_rows(vectors, columns_count):
    size = max(item.shape[1] for item in vectors)
    stacked = jnp.stack(
        [jnp.pad(item, ((0, 0), (0, size - item.shape[1]))) for item in vectors], axis=1
    )
    return jnp.pad(
        stacked, ((0, 0), (0, -stacked.shape[1] % 16), (0, columns_count - size))
    )


def per_device(
    tokens,
    cotangent,
    w_qkv,
    w_attn,
    w_fc,
    w_proj,
    bias_query,
    bias_value,
    bias_attn,
    gain_one,
    shift_one,
    gain_two,
    shift_two,
    bias_fc,
    bias_proj,
):
    ranks = lax.axis_size("seq")
    shards = lax.axis_size("dp")
    rank = lax.axis_index("seq")
    seqs, rows, model = tokens.shape
    length = rows * ranks
    width = model // ranks
    part = w_qkv.shape[0]
    hidden_part = w_proj.shape[0]
    units = hidden_part // ranks
    hidden_width = w_fc.shape[1] // ranks
    tokens_own = tokens.reshape(seqs * rows, model)
    cot_own = cotangent.reshape(seqs * rows, model)
    gather_columns = 4 * width
    *low_bits, top_bit = bits_up()

    def share_of(array, groups):
        size = array.shape[1] // (groups * ranks)
        return [
            lax.dynamic_slice_in_dim(array, (group * ranks + rank) * size, size, 1)
            for group in range(groups)
        ]

    vectors = [
        item.reshape(1, part)
        for item in (
            bias_query,
            bias_value,
            bias_attn,
            gain_one,
            shift_one,
            gain_two,
            shift_two,
            bias_proj,
        )
    ] + [item.reshape(1, units) for item in jnp.split(bias_fc, ranks)]
    packed = jnp.concatenate(
        [
            jnp.concatenate(share_of(w_qkv, 3) + share_of(w_attn, 1), axis=1),
            vector_rows(vectors, gather_columns)[0],
        ],
        axis=0,
    )

    token_far = swap(tokens, top_bit)
    steps = shards // 2
    middle_step = max(2, steps // 2)
    made = {}

    def feed_share():
        wide, tall = made["feed"]
        tall = lax.dynamic_slice_in_dim(tall, rank * units, units, 0)
        tall = tall.reshape(part, units * model // part)
        return jnp.concatenate(share_of(wide, shards) + [tall], axis=1)

    full = ring_gather(
        packed,
        {
            1: [("feed", lambda: (w_fc, w_proj))],
            middle_step: [("tokens", lambda: token_far)],
            steps - 1: [("share", feed_share)],
        },
        made,
    )
    token_blocks = gather_offsets(tokens, low_bits) + gather_offsets(made["tokens"], low_bits)
    second_gather = lax.all_gather(made["share"], "dp", axis=0)
    if units == part and hidden_width == model:
        feed_weights = second_gather.reshape(model, 2 * model)
    else:
        feed_weights = (
            second_gather[:, :, :hidden_width].reshape(model, hidden_width),
            second_gather[:, :, hidden_width:].reshape(hidden_width, model),
        )
    full_qkv = full[:, :part, : 3 * width].reshape(model, 3 * width)
    attn_columns = full[:, :part, 3 * width :].reshape(model, width)
    vector_block = full[:, part:].astype(F32)

    def vector(index):
        return vector_block[:, index, :part].reshape(model)

    query_bias = lax.dynamic_slice_in_dim(vector(0), rank * width, width)
    value_bias = lax.dynamic_slice_in_dim(vector(1), rank * width, width)
    attn_bias = vector(2)
    gain_first, shift_first, gain_second, shift_second, proj_bias = (
        vector(3),
        vector(4),
        vector(5),
        vector(6),
        vector(7),
    )
    fc_bias = lax.dynamic_index_in_dim(vector_block, 8 + rank, 1, keepdims=False)
    fc_bias = fc_bias[:, :units].reshape(hidden_width)
    half = ranks // 2
    joint_bias = jnp.concatenate([query_bias, jnp.zeros_like(query_bias), value_bias])
    normed, mixed = project(token_blocks, full_qkv, gain_first, shift_first, joint_bias)
    normed = normed.reshape(seqs * length, model)
    mixed = mixed.reshape(seqs, length, 3 * width)
    mixed, cot_sent, attn_columns, attn_far = lax.optimization_barrier(
        (mixed, cot_own, attn_columns, swap(attn_columns, top_bit))
    )
    cot_far = swap(cot_sent, top_bit)
    attended, logs = attend(mixed, width)
    sent = picked(attended, 1)
    _, cot_far, cot_near, attn_columns, attn_far = lax.optimization_barrier(
        (sent, cot_far, cot_own, attn_columns, attn_far)
    )
    near_cot = jnp.concatenate(gather_offsets(cot_near, low_bits), axis=0)
    far_cot = jnp.concatenate(gather_offsets(cot_far, low_bits), axis=0)

    arrived = [sent[0]] + [swap(sent[offset], offset) for offset in range(1, ranks)]
    attn_blocks = gather_offsets(attn_columns, low_bits) + gather_offsets(attn_far, low_bits)
    (full_attn,) = columns(attn_blocks, ((0, 1, width),), BF16)
    arrived, full_attn, near_cot, far_cot = lax.optimization_barrier(
        (arrived, full_attn, near_cot, far_cot)
    )
    (joined,) = columns(
        [item.reshape(seqs * rows, width) for item in arrived], ((0, 1, width),), BF16
    )

    inputs = tokens_own.astype(F32)
    middle = inputs + (dot_nn(joined, full_attn) + attn_bias)
    unit_two, inverse_two = row_stats(middle)
    normed_two = (unit_two * gain_second + shift_second).astype(BF16)
    near_blocks = gather_offsets(normed_two, low_bits)
    far_own = swap(normed_two, top_bit)
    feed_bias = fc_bias.reshape(1, hidden_width)
    near_active, near_grad, near_back, near_ahead, near_sum = feed(
        near_blocks, near_cot, feed_weights, feed_bias, hidden_width
    )
    far_own, near_active = lax.optimization_barrier((far_own, near_active))
    far_blocks = gather_offsets(far_own, low_bits)
    far_active, far_grad, far_back, far_ahead, far_sum = feed(
        far_blocks, far_cot, feed_weights, feed_bias, hidden_width
    )
    near_part = reduce_offsets(near_back, low_bits)
    far_part = reduce_offsets(far_back, low_bits).astype(BF16)
    far_part, far_active, far_grad = lax.optimization_barrier((far_part, far_active, far_grad))
    grad_normed_two = near_part.astype(F32) + swap(far_part, top_bit).astype(F32)
    near_two = jnp.concatenate(near_blocks, axis=0)
    far_two = jnp.concatenate(far_blocks, axis=0)

    upstream = cot_own.astype(F32)
    grad_w_proj = dot_tn(near_active, near_cot) + dot_tn(far_active, far_cot)
    grad_w_proj = grad_w_proj.astype(BF16).reshape(shards, part, units * model // part)
    grad_w_fc = dot_tn(near_two, near_grad) + dot_tn(far_two, far_grad)
    grad_w_fc = grad_w_fc.astype(BF16).reshape(shards, part, hidden_width)
    grad_bias_fc = (near_sum + far_sum).reshape(hidden_width)
    grad_bias_proj = jnp.sum(upstream, axis=0)
    first_parts = jnp.concatenate([grad_w_fc, grad_w_proj], axis=2)
    first_scatter = lax.psum_scatter(first_parts, "dp", scatter_dimension=0)
    grad_normed_two, _ = lax.optimization_barrier((grad_normed_two, first_parts))
    grad_gain_two = jnp.sum(grad_normed_two * unit_two, axis=0)
    grad_shift_two = jnp.sum(grad_normed_two, axis=0)
    grad_middle = upstream + norm_back(grad_normed_two, gain_second, unit_two, inverse_two)
    grad_branch = grad_middle.astype(BF16)
    grad_joined = dot_nt(grad_branch, full_attn).astype(BF16)
    grad_sent = picked(grad_joined.reshape(seqs, rows, model), 2)
    grad_arrived = [grad_sent[0]] + [
        swap(grad_sent[offset], offset) for offset in range(1, ranks)
    ]
    grad_attended = placed(grad_arrived, 1)

    ahead, _ = lax.optimization_barrier(((near_ahead, far_ahead), grad_branch))
    near_ahead, far_ahead = ahead
    ahead_far = reduce_offsets(far_ahead, low_bits).astype(BF16)
    grad_attn_part = picked(dot_tn(joined, grad_branch).astype(BF16), 1)
    attn_near = reduce_offsets(grad_attn_part[:half], low_bits)
    attn_far = reduce_offsets(grad_attn_part[half:], low_bits).astype(BF16)
    grad_attended, ahead_far, attn_far = lax.optimization_barrier(
        (grad_attended, ahead_far, attn_far)
    )
    ahead_far = swap(ahead_far, top_bit)
    attn_far = swap(attn_far, top_bit)
    ahead_part = reduce_offsets(near_ahead, low_bits)
    grad_w_attn = (attn_near.astype(F32) + attn_far.astype(F32)).astype(BF16)
    grad_bias_attn = jnp.sum(grad_branch, axis=0, dtype=F32)

    grad_mixed, column_sums = attend_back(mixed, attended, grad_attended, logs, width)
    grad_mixed = grad_mixed.reshape(seqs * length, 3 * width)
    back = dot_nt(grad_mixed, full_qkv).astype(BF16).reshape(seqs, length, model)
    back_blocks = [item.reshape(seqs * rows, model) for item in picked(back, 1)]
    back_blocks, grad_mixed = lax.optimization_barrier((back_blocks, grad_mixed))
    far_back = reduce_offsets(back_blocks[half:], low_bits).astype(BF16)
    grad_w_qkv = dot_tn(normed, grad_mixed)
    column_sums = jnp.sum(column_sums[:, 0], axis=0)
    qkv_values = full_qkv.astype(F32)
    grad_shift_one = jnp.sum(qkv_values * column_sums, axis=1)
    grad_gain_one = (
        jnp.sum(qkv_values * grad_w_qkv, axis=1) - shift_first * grad_shift_one
    ) / gain_first

    def spread(values):
        return lax.dynamic_update_slice_in_dim(
            jnp.zeros((model,), F32), values, rank * width, 0
        )

    grad_vectors = [
        item.reshape(shards, -1).astype(BF16)
        for item in (
            spread(column_sums[:width]),
            spread(column_sums[2 * width :]),
            grad_bias_attn,
            grad_gain_one,
            grad_shift_one,
            grad_gain_two,
            grad_shift_two,
            grad_bias_proj,
            grad_bias_fc,
        )
    ]
    last_parts = jnp.concatenate(
        [
            jnp.concatenate(
                [
                    grad_w_qkv.astype(BF16).reshape(shards, part, 3 * width),
                    grad_w_attn.reshape(shards, part, width),
                ],
                axis=2,
            ),
            vector_rows(grad_vectors, gather_columns),
        ],
        axis=1,
    )
    last_parts, far_back, near_back = lax.optimization_barrier(
        (last_parts, far_back, back_blocks[:half])
    )
    far_arrived = swap(far_back, top_bit)
    near_back = reduce_offsets(near_back, low_bits)
    made = {}
    last_scatter = ring_scatter(
        last_parts, {max(steps - 2, 1): [("scatter", lambda: first_scatter)]}, made
    )
    fed_far = swap(made["scatter"], top_bit)
    last_scatter = last_scatter.astype(BF16)
    far_arrived, fed_far, _ = lax.optimization_barrier((far_arrived, fed_far, last_scatter))
    grad_normed = near_back.astype(F32) + far_arrived.astype(F32)
    fed = gather_offsets(made["scatter"], low_bits) + gather_offsets(fed_far, low_bits)
    rest = gather_offsets(last_scatter)

    _, ahead_far = lax.optimization_barrier((grad_mixed, ahead_far))
    output = (middle + ahead_part.astype(F32) + ahead_far.astype(F32) + proj_bias).astype(BF16)
    unit_one, inverse_one = row_stats(inputs)
    grad_tokens = grad_middle + norm_back(grad_normed, gain_first, unit_one, inverse_one)

    (out_fc,) = columns(fed, ((0, shards, units),), F32)
    proj_blocks = [item[:, hidden_width:].reshape(units, model) for item in fed]
    out_proj = placed(proj_blocks, 0).astype(F32)
    out_qkv, out_attn = columns(rest, ((0, 3, width), (3 * width, 1, width)), F32, part)
    tails = [item[part:].astype(F32) for item in rest]
    summed = sum(tails)[:, :part]
    out_bias_fc = placed([item[8, :units] for item in tails], 0)

    def out_vector(index):
        return summed[index]

    return (
        output.reshape(seqs, rows, model),
        grad_tokens.reshape(seqs, rows, model),
        out_qkv,
        out_attn,
        out_fc,
        out_proj,
        out_vector(0),
        out_vector(1),
        out_vector(2),
        out_vector(3),
        out_vector(4),
        out_vector(5),
        out_vector(6),
        out_bias_fc,
        out_vector(7),
    )


def solution(mesh):
    token_spec = P("dp", "seq", None)
    in_specs = (token_spec,) * 2 + (P("dp", None),) * 4 + (P("dp"),) * 9
    out_specs = (token_spec,) * 2 + (P("dp", None),) * 4 + (P("dp"),) * 9
    return jax.shard_map(
        per_device, mesh=mesh, in_specs=in_specs, out_specs=out_specs, check_vma=False
    )
```

```python
import functools

import jax
import jax.numpy as jnp
from jax import lax
from jax.experimental import pallas as pl
from jax.experimental.pallas import tpu as pltpu
from jax.sharding import PartitionSpec as P

HEAD_DIM = 64
EPSILON = 1e-05
ROOT_COEF = 0.7978845608028654
SCALE = HEAD_DIM ** (-0.5)
BF16 = jnp.bfloat16
F32 = jnp.float32
LOG_ROWS = 8
VMEM_BYTES = 56 * 1024 * 1024


def gelu_tanh(values):
    return (
        0.5 * values * (1.0 + jnp.tanh(ROOT_COEF * (values + 0.044715 * values * values * values)))
    )


def dot_nn(left_side, right_side):
    return lax.dot_general(
        left_side, right_side, (((1,), (0,)), ((), ())), preferred_element_type=F32
    )


def dot_nt(left_side, right_side):
    return lax.dot_general(
        left_side, right_side, (((1,), (1,)), ((), ())), preferred_element_type=F32
    )


def dot_tn(left_side, right_side):
    return lax.dot_general(
        left_side, right_side, (((0,), (0,)), ((), ())), preferred_element_type=F32
    )


def project_kernel(rank_ref, *refs, parts):
    del rank_ref
    block_refs = refs[:parts]
    weight_ref, gain_ref, shift_ref, bias_ref, normed_ref, mixed_ref = refs[parts:]
    place = pl.program_id(0)
    values = block_refs[0][0]
    for part in range(1, parts):
        values = jnp.where(place == part, block_refs[part][0], values)
    values = values.astype(F32)
    centered = values - jnp.mean(values, axis=-1, keepdims=True)
    inverse = lax.rsqrt(jnp.mean(centered * centered, axis=-1, keepdims=True) + EPSILON)
    normed = (centered * inverse * gain_ref[...] + shift_ref[...]).astype(BF16)
    normed_ref[0, 0] = normed
    mixed_ref[0, 0] = (dot_nn(normed, weight_ref[...]) + bias_ref[...]).astype(BF16)


def project(blocks, weight, gain, shift, bias):
    seqs, rows, model = blocks[0].shape
    parts, wide = (len(blocks), weight.shape[1])
    block = min(256, rows)
    steps = rows // block

    def block_spec(part):
        def index_map(p, s, b, rank_ref):
            seq = jnp.where(p < part, 0, jnp.where(p > part, seqs - 1, s))
            row = jnp.where(p < part, 0, jnp.where(p > part, steps - 1, b))
            return (seq, row, 0)

        return pl.BlockSpec((1, block, model), index_map)

    def whole_spec(*shape):
        return pl.BlockSpec(shape, lambda p, s, b, rank_ref: (0, 0))

    def out_spec(columns_count):
        return pl.BlockSpec(
            (1, 1, block, columns_count),
            lambda p, s, b, rank_ref: (s, lax.bitwise_xor(rank_ref[0], p), b, 0),
        )

    return pl.pallas_call(
        functools.partial(project_kernel, parts=parts),
        grid_spec=pltpu.PrefetchScalarGridSpec(
            num_scalar_prefetch=1,
            grid=(parts, seqs, steps),
            in_specs=[block_spec(part) for part in range(parts)]
            + [
                whole_spec(model, wide),
                whole_spec(1, model),
                whole_spec(1, model),
                whole_spec(1, wide),
            ],
            out_specs=[out_spec(model), out_spec(wide)],
        ),
        out_shape=[
            jax.ShapeDtypeStruct((seqs, parts, rows, model), BF16),
            jax.ShapeDtypeStruct((seqs, parts, rows, wide), BF16),
        ],
        compiler_params=pltpu.CompilerParams(vmem_limit_bytes=VMEM_BYTES),
        cost_estimate=pl.CostEstimate(
            flops=4 * parts * seqs * rows * model * wide,
            bytes_accessed=parts * seqs * rows * (4 * model + 2 * wide) + 2 * model * wide,
            transcendentals=parts * seqs * rows,
        ),
    )(
        lax.axis_index("seq").astype(jnp.int32).reshape(1),
        *blocks,
        weight,
        gain.reshape(1, model),
        shift.reshape(1, model),
        bias.reshape(1, wide),
    )


def head_lanes(array, head):
    lanes = lax.broadcasted_iota(jnp.int32, array.shape, 1)
    owner = lax.shift_right_logical(lanes, 6)
    return jnp.where(owner == head, array.astype(F32), 0.0)


def attend_kernel(mixed_ref, out_ref, log_ref, *, block, width):
    length = mixed_ref.shape[1]
    heads = width // HEAD_DIM
    step = 4 if heads % 4 == 0 else 1
    for index in range(length // block):
        first, stop = index * block, (index + 1) * block
        query = mixed_ref[0, first:stop, 0:width]
        row_pos = lax.broadcasted_iota(jnp.int32, (block, block), 0)
        col_pos = lax.broadcasted_iota(jnp.int32, (block, block), 1)
        allowed = row_pos >= col_pos
        log_lanes = lax.broadcasted_iota(jnp.int32, (block, 128), 1)

        def one_head(head, carry):
            total, logs = carry
            masked = (head_lanes(query, head) * SCALE).astype(BF16)
            diagonal = dot_nt(masked, mixed_ref[0, first:stop, width : 2 * width])
            diagonal = jnp.where(allowed, diagonal, -1e30)
            largest = jnp.max(diagonal, axis=1, keepdims=True)
            if first:
                scores = dot_nt(masked, mixed_ref[0, 0:first, width : 2 * width])
                largest = jnp.maximum(largest, jnp.max(scores, axis=1, keepdims=True))
            weights = jnp.exp(diagonal - largest)
            row_total = jnp.sum(weights, axis=1, keepdims=True)
            mixed = dot_nn(
                weights.astype(BF16), mixed_ref[0, first:stop, 2 * width : 3 * width]
            )
            if first:
                weights = jnp.exp(scores - largest)
                row_total = row_total + jnp.sum(weights, axis=1, keepdims=True)
                mixed = mixed + dot_nn(
                    weights.astype(BF16), mixed_ref[0, 0:first, 2 * width : 3 * width]
                )
            total = total + head_lanes(mixed * (1.0 / row_total), head)
            logs = jnp.where(log_lanes == head, largest + jnp.log(row_total), logs)
            return (total, logs)

        def some_heads(group, carry):
            for inner in range(step):
                carry = one_head(group * step + inner, carry)
            return carry

        total, logs = lax.fori_loop(
            0,
            heads // step,
            some_heads,
            (jnp.zeros((block, width), F32), jnp.zeros((block, 128), F32)),
        )
        out_ref[0, first:stop, :] = total.astype(BF16)
        log_ref[0, :, first:stop] = jnp.transpose(logs)[0:LOG_ROWS]


def attend(mixed, width):
    seqs, length, _ = mixed.shape
    block = min(256, length)
    return pl.pallas_call(
        functools.partial(attend_kernel, block=block, width=width),
        grid=(seqs,),
        in_specs=[pl.BlockSpec((1, length, 3 * width), lambda s: (s, 0, 0))],
        out_specs=[
            pl.BlockSpec((1, length, width), lambda s: (s, 0, 0)),
            pl.BlockSpec((1, LOG_ROWS, length), lambda s: (s, 0, 0)),
        ],
        out_shape=[
            jax.ShapeDtypeStruct((seqs, length, width), BF16),
            jax.ShapeDtypeStruct((seqs, LOG_ROWS, length), F32),
        ],
        compiler_params=pltpu.CompilerParams(vmem_limit_bytes=VMEM_BYTES),
        cost_estimate=pl.CostEstimate(
            flops=28 * seqs * length * length * width,
            bytes_accessed=8 * seqs * length * width,
            transcendentals=seqs * length * length * width // HEAD_DIM // 2,
        ),
    )(mixed)


def attend_back_kernel(
    mixed_ref,
    out_ref,
    grad_ref,
    log_ref,
    result_ref,
    sum_ref,
    query_heads,
    key_heads,
    grad_heads,
    grad_query,
    grad_key,
    grad_value,
    inner_rows,
    *,
    block,
    width,
):
    length = mixed_ref.shape[1]
    heads = width // HEAD_DIM
    blocks = length // block
    owner = lax.shift_right_logical(lax.broadcasted_iota(jnp.int32, (LOG_ROWS, width), 1), 6)
    picks = (owner == lax.broadcasted_iota(jnp.int32, (LOG_ROWS, width), 0)).astype(F32)

    def prepare(index, carry):
        rows = pl.ds(pl.multiple_of(index * block, block), block)
        query = mixed_ref[0, rows, 0:width]
        key = mixed_ref[0, rows, width : 2 * width]
        grad = grad_ref[0, rows, :]
        for head in range(heads):
            query_heads[head, rows, :] = (head_lanes(query, head) * SCALE).astype(BF16)
            key_heads[head, rows, :] = head_lanes(key, head).astype(BF16)
            grad_heads[head, rows, :] = head_lanes(grad, head).astype(BF16)
        product = grad.astype(F32) * out_ref[0, rows, :].astype(F32)
        inner_rows[:, rows] = lax.dot_general(
            picks,
            product,
            (((1,), (1,)), ((), ())),
            precision=lax.Precision.HIGHEST,
            preferred_element_type=F32,
        )
        zeros = jnp.zeros((block, width), F32)
        grad_query[rows, :] = zeros
        grad_key[rows, :] = zeros
        grad_value[rows, :] = zeros
        return carry

    lax.fori_loop(0, blocks, prepare, 0)

    def tile(row_block, col_block, on_diagonal):
        rows = pl.ds(pl.multiple_of(row_block * block, block), block)
        cols = pl.ds(pl.multiple_of(col_block * block, block), block)
        key = mixed_ref[0, cols, width : 2 * width]
        value = mixed_ref[0, cols, 2 * width : 3 * width]
        add_query = add_key = add_value = None
        for head in range(heads):
            query = query_heads[head, rows, :]
            grad = grad_heads[head, rows, :]
            probs = jnp.exp(dot_nt(key, query) - log_ref[0, head : head + 1, rows])
            if on_diagonal:
                key_pos = lax.broadcasted_iota(jnp.int32, (block, block), 0)
                row_pos = lax.broadcasted_iota(jnp.int32, (block, block), 1)
                probs = jnp.where(row_pos >= key_pos, probs, 0.0)
            grad_probs = dot_nt(value, grad)
            grad_scores = (probs * (grad_probs - inner_rows[head : head + 1, rows])).astype(BF16)
            one_value = dot_nn(probs.astype(BF16), grad)
            one_key = dot_nn(grad_scores, query)
            one_query = dot_tn(grad_scores, key_heads[head, cols, :])
            add_value = one_value if head == 0 else add_value + one_value
            add_key = one_key if head == 0 else add_key + one_key
            add_query = one_query if head == 0 else add_query + one_query
        grad_value[cols, :] += add_value
        grad_key[cols, :] += add_key
        grad_query[rows, :] += add_query

    def row_step(row_block, carry):
        def col_step(col_block, inner_carry):
            tile(row_block, col_block, False)
            return inner_carry

        lax.fori_loop(0, row_block, col_step, 0)
        tile(row_block, row_block, True)
        return carry

    lax.fori_loop(0, blocks, row_step, 0)

    def finish(index, carry):
        rows = pl.ds(pl.multiple_of(index * block, block), block)
        pieces = (grad_query[rows, :] * SCALE, grad_key[rows, :], grad_value[rows, :])
        for place, piece in enumerate(pieces):
            piece = piece.astype(BF16)
            columns_here = slice(place * width, (place + 1) * width)
            result_ref[0, rows, columns_here] = piece
            sum_ref[0, 0:1, columns_here] += jnp.sum(piece.astype(F32), axis=0, keepdims=True)
        return carry

    sum_ref[...] = jnp.zeros_like(sum_ref)
    lax.fori_loop(0, blocks, finish, 0)


def attend_back(mixed, attended, grad_attended, logs, width):
    seqs, length, _ = mixed.shape
    heads = width // HEAD_DIM
    block = min(512, length)
    return pl.pallas_call(
        functools.partial(attend_back_kernel, block=block, width=width),
        grid=(seqs,),
        in_specs=[
            pl.BlockSpec((1, length, 3 * width), lambda s: (s, 0, 0)),
            pl.BlockSpec((1, length, width), lambda s: (s, 0, 0)),
            pl.BlockSpec((1, length, width), lambda s: (s, 0, 0)),
            pl.BlockSpec((1, LOG_ROWS, length), lambda s: (s, 0, 0)),
        ],
        out_specs=[
            pl.BlockSpec((1, length, 3 * width), lambda s: (s, 0, 0)),
            pl.BlockSpec((1, 8, 3 * width), lambda s: (s, 0, 0)),
        ],
        out_shape=[
            jax.ShapeDtypeStruct((seqs, length, 3 * width), BF16),
            jax.ShapeDtypeStruct((seqs, 8, 3 * width), F32),
        ],
        scratch_shapes=[
            pltpu.VMEM((heads, length, width), BF16),
            pltpu.VMEM((heads, length, width), BF16),
            pltpu.VMEM((heads, length, width), BF16),
            pltpu.VMEM((length, width), F32),
            pltpu.VMEM((length, width), F32),
            pltpu.VMEM((length, width), F32),
            pltpu.VMEM((LOG_ROWS, length), F32),
        ],
        compiler_params=pltpu.CompilerParams(vmem_limit_bytes=VMEM_BYTES),
        cost_estimate=pl.CostEstimate(
            flops=56 * seqs * length * length * width,
            bytes_accessed=16 * seqs * length * width,
            transcendentals=seqs * length * length * width // HEAD_DIM // 2,
        ),
    )(mixed, attended, grad_attended, logs)


def feed_kernel(*refs, parts, steps):
    normed_refs, rest = (refs[:parts], refs[parts:])
    cot_ref, fc_ref, proj_ref, bias_ref, active_ref, grad_ref = rest[:6]
    back_refs, ahead_refs = (rest[6 : 6 + parts], rest[6 + parts : 6 + 2 * parts])
    sum_ref = rest[6 + 2 * parts]
    index = pl.program_id(0)
    normed = normed_refs[0][...]
    for place in range(1, parts):
        normed = jnp.where(index >= place * steps, normed_refs[place][...], normed)
    hidden = dot_nn(normed, fc_ref[...]) + bias_ref[...]
    grad_active = dot_nt(cot_ref[...], proj_ref[...])
    square = hidden * hidden
    curve = jnp.tanh(ROOT_COEF * hidden * (1.0 + 0.044715 * square))
    half = 0.5 + 0.5 * curve
    active = (hidden * half).astype(BF16)
    slope = half + hidden * (0.5 - 0.5 * curve * curve) * (
        ROOT_COEF + (3.0 * 0.044715 * ROOT_COEF) * square
    )
    grad = (grad_active * slope).astype(BF16)
    active_ref[...] = active
    grad_ref[...] = grad
    back = dot_nt(grad, fc_ref[...]).astype(BF16)
    ahead = dot_nn(active, proj_ref[...]).astype(BF16)
    for place in range(parts):

        @pl.when(jnp.logical_and(index >= place * steps, index < (place + 1) * steps))
        def _(place=place):
            back_refs[place][...] = back
            ahead_refs[place][...] = ahead

    sums = jnp.sum(grad.astype(F32), axis=0, keepdims=True)

    @pl.when(index == 0)
    def _():
        sum_ref[...] = jnp.zeros_like(sum_ref)

    sum_ref[...] += sums


def feed(blocks, cotangent, weights, bias, width):
    rows, model = blocks[0].shape
    parts = len(blocks)
    block = min(256, rows)
    steps = rows // block

    def part_spec(place):
        return pl.BlockSpec((block, model), lambda i: (jnp.clip(i - place * steps, 0, steps - 1), 0))

    part_specs = [part_spec(place) for place in range(parts)]
    part_shapes = [jax.ShapeDtypeStruct((rows, model), BF16)] * parts
    wide_spec = pl.BlockSpec((block, width), lambda i: (i, 0))
    wide_shape = jax.ShapeDtypeStruct((parts * rows, width), BF16)
    if isinstance(weights, tuple):
        share_fc, share_proj = weights
        proj_place = 0
    else:
        share_fc = share_proj = weights
        proj_place = 1
    results = pl.pallas_call(
        functools.partial(feed_kernel, parts=parts, steps=steps),
        grid=(parts * steps,),
        in_specs=part_specs
        + [
            pl.BlockSpec((block, model), lambda i: (i, 0)),
            pl.BlockSpec((model, width), lambda i: (0, 0)),
            pl.BlockSpec((width, model), lambda i: (0, proj_place)),
            pl.BlockSpec((1, width), lambda i: (0, 0)),
        ],
        out_specs=[wide_spec, wide_spec]
        + part_specs
        + part_specs
        + [pl.BlockSpec((1, width), lambda i: (0, 0))],
        out_shape=[wide_shape, wide_shape]
        + part_shapes
        + part_shapes
        + [jax.ShapeDtypeStruct((1, width), F32)],
        compiler_params=pltpu.CompilerParams(vmem_limit_bytes=VMEM_BYTES),
        cost_estimate=pl.CostEstimate(
            flops=14 * parts * rows * model * width,
            bytes_accessed=parts * rows * (8 * model + 4 * width) + 4 * model * width,
            transcendentals=parts * rows * width,
        ),
    )(*blocks, cotangent, share_fc, share_proj, bias)
    back, ahead = (results[2 : 2 + parts], results[2 + parts : 2 + 2 * parts])
    return results[0], results[1], back, ahead, results[2 + 2 * parts]


def ring_order(shards):
    fast = 1
    while fast * fast * 4 <= shards:
        fast *= 2
    slow = shards // fast
    if fast == 1:
        return list(range(shards))
    path = [row * fast for row in range(slow)]
    for row in reversed(range(slow)):
        line = range(1, fast) if (slow - 1 - row) % 2 == 0 else reversed(range(1, fast))
        path += [row * fast + place for place in line]
    return path


def ring_move(array, towards):
    order = ring_order(lax.axis_size("dp"))
    shards = len(order)
    pairs = [(order[i], order[(i + towards) % shards]) for i in range(shards)]
    return lax.ppermute(array, "dp", pairs)


def ring_lookup(distance):
    order = ring_order(lax.axis_size("dp"))
    shards = len(order)
    own = lax.axis_index("dp")
    found = jnp.int32(order[distance % shards])
    for place in range(1, shards):
        found = jnp.where(own == order[place], order[(place + distance) % shards], found)
    return found


def ring_gather(share, ties, made):
    shards = lax.axis_size("dp")
    full = jnp.zeros((shards,) + share.shape, share.dtype)
    full = lax.dynamic_update_index_in_dim(full, share, lax.axis_index("dp"), 0)
    upward = downward = share
    for step in range(1, shards // 2 + 1):
        upward = ring_move(upward, 1)
        if 2 * step < shards:
            downward = ring_move(downward, -1)
        full = lax.dynamic_update_index_in_dim(full, upward, ring_lookup(-step), 0)
        if 2 * step < shards:
            full = lax.dynamic_update_index_in_dim(full, downward, ring_lookup(step), 0)
        for name, make in ties.get(step, ()):
            upward, made[name] = lax.optimization_barrier((upward, make()))
    return full


def ring_scatter(parts, ties, made):
    shards = parts.shape[0]
    half = shards // 2

    def own(distance):
        return lax.dynamic_index_in_dim(parts, ring_lookup(distance), 0, keepdims=False)

    downward = upward = None
    for distance in range(half, 0, -1):
        held = own(-distance)
        if downward is not None:
            held = (held.astype(F32) + downward.astype(F32)).astype(BF16)
        for name, make in ties.get(distance, ()):
            held, made[name] = lax.optimization_barrier((held, make()))
        downward = ring_move(held, -1)
        if distance < half or 2 * half < shards:
            held = own(distance)
            if upward is not None:
                held = (held.astype(F32) + upward.astype(F32)).astype(BF16)
            upward = ring_move(held, 1)
    total = own(0).astype(F32) + downward.astype(F32)
    return total if upward is None else total + upward.astype(F32)


def swap(array, offset):
    ranks = lax.axis_size("seq")
    return lax.ppermute(array, "seq", [(rank, rank ^ offset) for rank in range(ranks)])


def bits_up():
    ranks, bits, bit = (lax.axis_size("seq"), [], 1)
    while bit < ranks:
        bits.append(bit)
        bit *= 2
    return bits


def gather_offsets(array, bits=None):
    found = {0: array}
    for bit in reversed(bits_up() if bits is None else bits):
        for offset in sorted(found):
            found[offset | bit] = swap(found[offset], bit)
    return [found[offset] for offset in range(len(found))]


def reduce_offsets(blocks, bits=None):
    left = dict(enumerate(blocks))
    for bit in bits_up() if bits is None else bits:
        for offset in sorted(left, reverse=True):
            if offset & bit:
                arrived = swap(left.pop(offset).astype(BF16), bit)
                left[offset ^ bit] = left[offset ^ bit].astype(F32) + arrived.astype(F32)
    return left[0]


def placed(blocks, axis):
    rank = lax.axis_index("seq")
    size = blocks[0].shape[axis]
    shape = list(blocks[0].shape)
    shape[axis] = size * len(blocks)
    full = jnp.zeros(shape, blocks[0].dtype)
    for offset, block in enumerate(blocks):
        full = lax.dynamic_update_slice_in_dim(full, block, (rank ^ offset) * size, axis)
    return full


def picked(array, axis):
    rank, ranks = (lax.axis_index("seq"), lax.axis_size("seq"))
    size = array.shape[axis] // ranks
    return [
        lax.dynamic_slice_in_dim(array, (rank ^ offset) * size, size, axis)
        for offset in range(ranks)
    ]


def columns_kernel(rank_ref, *refs, pieces, ranks):
    blocks, fulls = (refs[:ranks], refs[ranks:])
    for offset, block_ref in enumerate(blocks):
        owner = lax.bitwise_xor(rank_ref[0, 0], offset)
        for (first, groups, size), full_ref in zip(pieces, fulls):
            for group in range(groups):
                start = pl.multiple_of((owner + group * ranks) * size, size)
                place = first + group * size
                piece = block_ref[0 : full_ref.shape[0], place : place + size]
                full_ref[:, pl.ds(start, size)] = piece.astype(full_ref.dtype)


def columns(blocks, pieces, dtype, rows=None):
    rows = blocks[0].shape[0] if rows is None else rows
    ranks = len(blocks)
    rank = lax.axis_index("seq")
    if any(size % 128 for _, _, size in pieces):
        results = []
        for first, groups, size in pieces:
            shaped = [
                block[:rows, first : first + groups * size].reshape(rows, groups, 1, size)
                for block in blocks
            ]
            results.append(placed(shaped, 2).reshape(rows, ranks * groups * size).astype(dtype))
        return results
    wide = sum(groups * size for _, groups, size in pieces) * ranks
    return pl.pallas_call(
        functools.partial(columns_kernel, pieces=pieces, ranks=ranks),
        in_specs=[pl.BlockSpec(memory_space=pltpu.SMEM)]
        + [pl.BlockSpec(memory_space=pltpu.VMEM)] * ranks,
        out_specs=[pl.BlockSpec(memory_space=pltpu.VMEM)] * len(pieces),
        out_shape=[
            jax.ShapeDtypeStruct((rows, ranks * groups * size), dtype)
            for _, groups, size in pieces
        ],
        compiler_params=pltpu.CompilerParams(vmem_limit_bytes=VMEM_BYTES),
        cost_estimate=pl.CostEstimate(
            flops=rows * wide, bytes_accessed=6 * rows * wide, transcendentals=0
        ),
    )(rank.astype(jnp.int32).reshape(1, 1), *blocks)


def row_stats(values):
    average = jnp.mean(values, axis=-1, keepdims=True)
    centered = values - average
    variance = jnp.mean(centered * centered, axis=-1, keepdims=True)
    inverse = lax.rsqrt(variance + EPSILON)
    return centered * inverse, inverse


def norm_back(incoming, gain, unit, inverse):
    scaled = incoming * gain
    first = jnp.mean(scaled, axis=-1, keepdims=True)
    second = jnp.mean(scaled * unit, axis=-1, keepdims=True)
    return inverse * (scaled - first - unit * second)


def vector_rows(vectors, columns_count):
    size = max(item.shape[1] for item in vectors)
    stacked = jnp.stack(
        [jnp.pad(item, ((0, 0), (0, size - item.shape[1]))) for item in vectors], axis=1
    )
    return jnp.pad(
        stacked, ((0, 0), (0, -stacked.shape[1] % 16), (0, columns_count - size))
    )


def per_device(
    tokens,
    cotangent,
    w_qkv,
    w_attn,
    w_fc,
    w_proj,
    bias_query,
    bias_value,
    bias_attn,
    gain_one,
    shift_one,
    gain_two,
    shift_two,
    bias_fc,
    bias_proj,
):
    ranks = lax.axis_size("seq")
    shards = lax.axis_size("dp")
    rank = lax.axis_index("seq")
    seqs, rows, model = tokens.shape
    length = rows * ranks
    width = model // ranks
    part = w_qkv.shape[0]
    hidden_part = w_proj.shape[0]
    units = hidden_part // ranks
    hidden_width = w_fc.shape[1] // ranks
    tokens_own = tokens.reshape(seqs * rows, model)
    cot_own = cotangent.reshape(seqs * rows, model)
    gather_columns = 4 * width
    *low_bits, top_bit = bits_up()

    def share_of(array, groups):
        size = array.shape[1] // (groups * ranks)
        return [
            lax.dynamic_slice_in_dim(array, (group * ranks + rank) * size, size, 1)
            for group in range(groups)
        ]

    vectors = [
        item.reshape(1, part)
        for item in (
            bias_query,
            bias_value,
            bias_attn,
            gain_one,
            shift_one,
            gain_two,
            shift_two,
            bias_proj,
        )
    ] + [item.reshape(1, units) for item in jnp.split(bias_fc, ranks)]
    packed = jnp.concatenate(
        [
            jnp.concatenate(share_of(w_qkv, 3) + share_of(w_attn, 1), axis=1),
            vector_rows(vectors, gather_columns)[0],
        ],
        axis=0,
    )

    token_far = swap(tokens, top_bit)
    steps = shards // 2
    middle_step = max(2, steps // 2)
    made = {}

    def feed_share():
        wide, tall = made["feed"]
        tall = lax.dynamic_slice_in_dim(tall, rank * units, units, 0)
        tall = tall.reshape(part, units * model // part)
        return jnp.concatenate(share_of(wide, shards) + [tall], axis=1)

    full = ring_gather(
        packed,
        {
            1: [("feed", lambda: (w_fc, w_proj))],
            middle_step: [("tokens", lambda: token_far)],
            steps - 1: [("share", feed_share)],
        },
        made,
    )
    token_blocks = gather_offsets(tokens, low_bits) + gather_offsets(made["tokens"], low_bits)
    second_gather = lax.all_gather(made["share"], "dp", axis=0)
    if units == part and hidden_width == model:
        feed_weights = second_gather.reshape(model, 2 * model)
    else:
        feed_weights = (
            second_gather[:, :, :hidden_width].reshape(model, hidden_width),
            second_gather[:, :, hidden_width:].reshape(hidden_width, model),
        )
    full_qkv = full[:, :part, : 3 * width].reshape(model, 3 * width)
    attn_columns = full[:, :part, 3 * width :].reshape(model, width)
    vector_block = full[:, part:].astype(F32)

    def vector(index):
        return vector_block[:, index, :part].reshape(model)

    query_bias = lax.dynamic_slice_in_dim(vector(0), rank * width, width)
    value_bias = lax.dynamic_slice_in_dim(vector(1), rank * width, width)
    attn_bias = vector(2)
    gain_first, shift_first, gain_second, shift_second, proj_bias = (
        vector(3),
        vector(4),
        vector(5),
        vector(6),
        vector(7),
    )
    fc_bias = lax.dynamic_index_in_dim(vector_block, 8 + rank, 1, keepdims=False)
    fc_bias = fc_bias[:, :units].reshape(hidden_width)
    half = ranks // 2
    joint_bias = jnp.concatenate([query_bias, jnp.zeros_like(query_bias), value_bias])
    normed, mixed = project(token_blocks, full_qkv, gain_first, shift_first, joint_bias)
    normed = normed.reshape(seqs * length, model)
    mixed = mixed.reshape(seqs, length, 3 * width)
    mixed, cot_sent, attn_columns, attn_far = lax.optimization_barrier(
        (mixed, cot_own, attn_columns, swap(attn_columns, top_bit))
    )
    cot_far = swap(cot_sent, top_bit)
    attended, logs = attend(mixed, width)
    sent = picked(attended, 1)
    arrived = [sent[0]] + [swap(sent[offset], offset) for offset in range(1, ranks)]
    _, cot_far, cot_near, attn_columns, attn_far = lax.optimization_barrier(
        (arrived[1], cot_far, cot_own, attn_columns, attn_far)
    )
    near_cot = jnp.concatenate(gather_offsets(cot_near, low_bits), axis=0)
    far_cot = jnp.concatenate(gather_offsets(cot_far, low_bits), axis=0)

    attn_blocks = gather_offsets(attn_columns, low_bits) + gather_offsets(attn_far, low_bits)
    (full_attn,) = columns(attn_blocks, ((0, 1, width),), BF16)
    arrived, full_attn, near_cot, far_cot = lax.optimization_barrier(
        (arrived, full_attn, near_cot, far_cot)
    )
    (joined,) = columns(
        [item.reshape(seqs * rows, width) for item in arrived], ((0, 1, width),), BF16
    )

    inputs = tokens_own.astype(F32)
    middle = inputs + (dot_nn(joined, full_attn) + attn_bias)
    unit_two, inverse_two = row_stats(middle)
    normed_two = (unit_two * gain_second + shift_second).astype(BF16)
    near_blocks = gather_offsets(normed_two, low_bits)
    far_own = swap(normed_two, top_bit)
    feed_bias = fc_bias.reshape(1, hidden_width)
    near_active, near_grad, near_back, near_ahead, near_sum = feed(
        near_blocks, near_cot, feed_weights, feed_bias, hidden_width
    )
    far_own, near_active = lax.optimization_barrier((far_own, near_active))
    far_blocks = gather_offsets(far_own, low_bits)
    far_active, far_grad, far_back, far_ahead, far_sum = feed(
        far_blocks, far_cot, feed_weights, feed_bias, hidden_width
    )
    near_part = reduce_offsets(near_back, low_bits)
    far_part = reduce_offsets(far_back, low_bits).astype(BF16)
    far_part, far_active, far_grad = lax.optimization_barrier((far_part, far_active, far_grad))
    grad_normed_two = near_part.astype(F32) + swap(far_part, top_bit).astype(F32)
    near_two = jnp.concatenate(near_blocks, axis=0)
    far_two = jnp.concatenate(far_blocks, axis=0)

    upstream = cot_own.astype(F32)
    grad_w_proj = dot_tn(near_active, near_cot) + dot_tn(far_active, far_cot)
    grad_w_proj = grad_w_proj.astype(BF16).reshape(shards, part, units * model // part)
    grad_w_fc = dot_tn(near_two, near_grad) + dot_tn(far_two, far_grad)
    grad_w_fc = grad_w_fc.astype(BF16).reshape(shards, part, hidden_width)
    grad_bias_fc = (near_sum + far_sum).reshape(hidden_width)
    grad_bias_proj = jnp.sum(upstream, axis=0)
    first_parts = jnp.concatenate([grad_w_fc, grad_w_proj], axis=2)
    first_scatter = lax.psum_scatter(first_parts, "dp", scatter_dimension=0)
    grad_normed_two, _ = lax.optimization_barrier((grad_normed_two, first_parts))
    grad_gain_two = jnp.sum(grad_normed_two * unit_two, axis=0)
    grad_shift_two = jnp.sum(grad_normed_two, axis=0)
    grad_middle = upstream + norm_back(grad_normed_two, gain_second, unit_two, inverse_two)
    grad_branch = grad_middle.astype(BF16)
    grad_joined = dot_nt(grad_branch, full_attn).astype(BF16)
    grad_sent = picked(grad_joined.reshape(seqs, rows, model), 2)
    grad_arrived = [grad_sent[0]] + [
        swap(grad_sent[offset], offset) for offset in range(1, ranks)
    ]
    grad_attended = placed(grad_arrived, 1)

    ahead, _ = lax.optimization_barrier(((near_ahead, far_ahead), grad_branch))
    near_ahead, far_ahead = ahead
    ahead_far = reduce_offsets(far_ahead, low_bits).astype(BF16)
    grad_attn_part = picked(dot_tn(joined, grad_branch).astype(BF16), 1)
    attn_near = reduce_offsets(grad_attn_part[:half], low_bits)
    attn_far = reduce_offsets(grad_attn_part[half:], low_bits).astype(BF16)
    grad_attended, ahead_far, attn_far = lax.optimization_barrier(
        (grad_attended, ahead_far, attn_far)
    )
    ahead_far = swap(ahead_far, top_bit)
    attn_far = swap(attn_far, top_bit)
    ahead_part = reduce_offsets(near_ahead, low_bits)
    grad_bias_attn = jnp.sum(grad_branch, axis=0, dtype=F32)

    grad_mixed, column_sums = attend_back(mixed, attended, grad_attended, logs, width)
    grad_mixed, attn_far, ahead_far = lax.optimization_barrier((grad_mixed, attn_far, ahead_far))
    grad_w_attn = (attn_near.astype(F32) + attn_far.astype(F32)).astype(BF16)
    grad_mixed = grad_mixed.reshape(seqs * length, 3 * width)
    back = dot_nt(grad_mixed, full_qkv).astype(BF16).reshape(seqs, length, model)
    back_blocks = [item.reshape(seqs * rows, model) for item in picked(back, 1)]
    back_blocks, grad_mixed = lax.optimization_barrier((back_blocks, grad_mixed))
    far_back = reduce_offsets(back_blocks[half:], low_bits).astype(BF16)
    grad_w_qkv = dot_tn(normed, grad_mixed)
    column_sums = jnp.sum(column_sums[:, 0], axis=0)
    qkv_values = full_qkv.astype(F32)
    grad_shift_one = jnp.sum(qkv_values * column_sums, axis=1)
    grad_gain_one = (
        jnp.sum(qkv_values * grad_w_qkv, axis=1) - shift_first * grad_shift_one
    ) / gain_first

    def spread(values):
        return lax.dynamic_update_slice_in_dim(
            jnp.zeros((model,), F32), values, rank * width, 0
        )

    grad_vectors = [
        item.reshape(shards, -1).astype(BF16)
        for item in (
            spread(column_sums[:width]),
            spread(column_sums[2 * width :]),
            grad_bias_attn,
            grad_gain_one,
            grad_shift_one,
            grad_gain_two,
            grad_shift_two,
            grad_bias_proj,
            grad_bias_fc,
        )
    ]
    last_parts = jnp.concatenate(
        [
            jnp.concatenate(
                [
                    grad_w_qkv.astype(BF16).reshape(shards, part, 3 * width),
                    grad_w_attn.reshape(shards, part, width),
                ],
                axis=2,
            ),
            vector_rows(grad_vectors, gather_columns),
        ],
        axis=1,
    )
    last_parts, far_back, near_back = lax.optimization_barrier(
        (last_parts, far_back, back_blocks[:half])
    )
    far_arrived = swap(far_back, top_bit)
    near_back = reduce_offsets(near_back, low_bits)
    made = {}
    last_scatter = ring_scatter(
        last_parts, {max(steps - 2, 1): [("scatter", lambda: first_scatter)]}, made
    )
    fed_far = swap(made["scatter"], top_bit)
    last_scatter = last_scatter.astype(BF16)
    far_arrived, fed_far, _ = lax.optimization_barrier((far_arrived, fed_far, last_scatter))
    grad_normed = near_back.astype(F32) + far_arrived.astype(F32)
    fed = gather_offsets(made["scatter"], low_bits) + gather_offsets(fed_far, low_bits)
    rest = gather_offsets(last_scatter)

    output = (middle + ahead_part.astype(F32) + ahead_far.astype(F32) + proj_bias).astype(BF16)
    unit_one, inverse_one = row_stats(inputs)
    grad_tokens = grad_middle + norm_back(grad_normed, gain_first, unit_one, inverse_one)

    (out_fc,) = columns(fed, ((0, shards, units),), F32)
    proj_blocks = [item[:, hidden_width:].reshape(units, model) for item in fed]
    out_proj = placed(proj_blocks, 0).astype(F32)
    out_qkv, out_attn = columns(rest, ((0, 3, width), (3 * width, 1, width)), F32, part)
    tails = [item[part:].astype(F32) for item in rest]
    summed = sum(tails)[:, :part]
    out_bias_fc = placed([item[8, :units] for item in tails], 0)

    def out_vector(index):
        return summed[index]

    return (
        output.reshape(seqs, rows, model),
        grad_tokens.reshape(seqs, rows, model),
        out_qkv,
        out_attn,
        out_fc,
        out_proj,
        out_vector(0),
        out_vector(1),
        out_vector(2),
        out_vector(3),
        out_vector(4),
        out_vector(5),
        out_vector(6),
        out_bias_fc,
        out_vector(7),
    )


def solution(mesh):
    token_spec = P("dp", "seq", None)
    in_specs = (token_spec,) * 2 + (P("dp", None),) * 4 + (P("dp"),) * 9
    out_specs = (token_spec,) * 2 + (P("dp", None),) * 4 + (P("dp"),) * 9
    return jax.shard_map(
        per_device, mesh=mesh, in_specs=in_specs, out_specs=out_specs, check_vma=False
    )
```
